32 devices in a mesh: circ: 4 (over z), radax: 8 (over y, x, core).
Axes of the slice: x: 2, y: 2, z: 4, core: 2. Of those that a mesh axis runs over, the one named last changes fastest.
Arguments:
- right_side: float32 [2048, 2048], P('circ', 'radax'), may hold values from -150 to 150
- coef_rotor: float32 [2048, 2048], P('circ', 'radax'), may hold values from 1.5 to 15
- coef_stator: float32 [2048, 2048], P('circ', 'radax'), may hold values from 1.5 to 15
- mortar_rows: int32 [2048], P('circ'), may hold values from 0 to 2047, as said below
- mortar_weight: float32 [2048], P('circ'), may hold values from 0.1 to 0.9
Outputs:
- solution_field: float32 [2048, 2048], P('circ', 'radax')
- residual: float32 [2048, 2048], P('circ', 'radax')
The draws below stay inside these ranges and needn't reach their ends.
Inputs may be any that keep to these rules, and one draw needn't show every extreme that they name: (mortar_rows[s] - s - 1280) taken modulo 2048 lies in -3 to 3, and both ends occur.
All inputs are finite; a program needn't handle non-finite values.
Results may differ from the reference program's by a relative error of at most 0.0002.
Values sent between devices are 32-bit elements; how exact they have to be, the bound alone decides.
No kernel may reach another device: no remote copies, remote signals or barrier semaphores. Data moves between devices by JAX's collectives and lax.ppermute only.
A program may use at most 64 MiB of HBM per device.

```python
import math
import jax
import jax.numpy as jnp

W = 256
REACH = 3
SLIDE = 1280
NROWS = 2048
WG = 2048
N_RADAX = 8


def draw_right_side(key, part):
    key_noise = jax.random.fold_in(key, 11)
    key_rows = jax.random.fold_in(key, 12)
    key_cols = jax.random.fold_in(key, 13)
    row_scale = jnp.exp(jax.random.uniform(key_rows, (NROWS, 1), jnp.float32, 0.0, 2.302585))
    col_scale = jnp.exp(jax.random.uniform(key_cols, (1, WG), jnp.float32, 0.0, 2.302585))
    ramp = 1.0 + 2.0 * jnp.arange(NROWS, dtype=jnp.float32)[:, None] / NROWS
    noise = jax.random.truncated_normal(key_noise, -4.0, 4.0, (NROWS, WG), jnp.float32)
    return (0.1 * noise * row_scale * col_scale * ramp).astype(jnp.float32)


def draw_mortar_rows(key, part):
    key_delta = jax.random.fold_in(key, 21)
    delta = jax.random.randint(key_delta, (NROWS,), -REACH, REACH + 1, jnp.int32)
    delta = delta.at[0].set(-REACH).at[1].set(REACH)
    base = jnp.arange(NROWS, dtype=jnp.int32)
    return jnp.mod(base + SLIDE + delta, NROWS).astype(jnp.int32)


def levels(own_key, extent, shards, smallest, high):
    def one(position, blocks):
        draws = jax.random.uniform(jax.random.fold_in(jax.random.fold_in(own_key, 6), position), (blocks,), jnp.float32, smallest / len(shards), high / len(shards))
        return jnp.repeat(jnp.exp(draws), extent[position] // blocks).reshape((-1,) + (1,) * (len(extent) - position - 1))

    level = one(*shards[0])
    for cut in shards[1:]:
        level = level * one(*cut)
    return level


def setup_inputs(seed: int = 0) -> dict:
    keys = jax.random.split(jax.random.key(seed), 6)
    return {
        "right_side": draw_right_side(jax.random.fold_in(keys[5], 71), 0),
        "coef_rotor": jnp.clip(jnp.exp(math.log(15.0) - 2.3025851 * jax.random.uniform(keys[1], (NROWS, WG), jnp.float32) ** levels(keys[1], (NROWS, WG), ((0, 4), (1, 8)), -0.2, 0.2)), 1.5, 15.0),
        "coef_stator": jnp.clip(jnp.exp(math.log(15.0) - 2.3025851 * jax.random.uniform(keys[2], (NROWS, WG), jnp.float32) ** levels(keys[2], (NROWS, WG), ((0, 4), (1, 8)), -0.2, 0.2)), 1.5, 15.0),
        "mortar_rows": draw_mortar_rows(jax.random.fold_in(keys[5], 71), 0),
        "mortar_weight": jnp.clip(0.1 + 0.79999997 * jax.random.uniform(keys[4], (NROWS,), jnp.float32) ** levels(keys[4], (NROWS,), ((0, 4),), -0.2, 0.2), 0.1, 0.9),
    }


def stencil(grid_field, coef):
    above = jnp.roll(grid_field, 1, axis=0)
    below = jnp.roll(grid_field, -1, axis=0)
    blocks = grid_field.reshape(grid_field.shape[0], N_RADAX, W)
    padded = jnp.pad(blocks, ((0, 0), (0, 0), (1, 1)))
    beside = (padded[:, :, :-2] + padded[:, :, 2:]).reshape(grid_field.shape)
    return coef * grid_field - 0.25 * (above + below + beside)


def operator(trace, coef_rotor, coef_stator, first_rows, next_rows, weight):
    projected = weight * trace[first_rows] + (1.0 - weight) * trace[next_rows]
    response = stencil(projected, coef_stator)
    returned = jnp.zeros_like(trace).at[first_rows].add(weight * response)
    returned = returned.at[next_rows].add((1.0 - weight) * response)
    return stencil(trace, coef_rotor) + returned


def reference(right_side, coef_rotor, coef_stator, mortar_rows, mortar_weight):
    first_rows = mortar_rows.astype(jnp.int32)
    next_rows = jnp.mod(first_rows + 1, NROWS).astype(jnp.int32)
    weight = mortar_weight[:, None]
    image = operator(right_side, coef_rotor, coef_stator, first_rows, next_rows, weight)
    second = operator(image, coef_rotor, coef_stator, first_rows, next_rows, weight)
    cross_one = jnp.sum(right_side * image)
    cross_two = jnp.sum(right_side * second)
    gram_pp = jnp.sum(image * image)
    gram_pq = jnp.sum(image * second)
    gram_qq = jnp.sum(second * second)
    determinant = gram_pp * gram_qq - gram_pq * gram_pq
    coeff_one = (gram_qq * cross_one - gram_pq * cross_two) / determinant
    coeff_two = (gram_pp * cross_two - gram_pq * cross_one) / determinant
    solution_field = coeff_one * right_side + coeff_two * image
    residual = right_side - coeff_one * image - coeff_two * second
    return solution_field, residual
```

```python
import functools

import jax
import jax.numpy as jnp
from jax import lax
from jax.experimental import pallas as pl
from jax.experimental.pallas import tpu as pltpu
from jax.sharding import PartitionSpec as P

W = 256
REACH = 3
SLIDE = 1280

LANES = 128
SUB = 8
SPAN = 2 * (REACH + 1)
HALO = 2 * SPAN
TAPS = range(-REACH, REACH + 2)
VMEM = pl.BlockSpec(memory_space=pltpu.VMEM)
PARAMS = pltpu.CompilerParams(vmem_limit_bytes=40 << 20)


def shifted(block, distance):
    count = lax.axis_size("circ")
    route = [((i - distance) % count, i) for i in range(count)]
    return lax.ppermute(block, "circ", route)


def up8(count):
    return -(-count // SUB) * SUB


def chunk_of(rows, most=136):
    return max(c for c in range(SUB, most + 1, SUB) if rows % c == 0)


def for_chunks(first, rows, body, init=None):
    step = chunk_of(rows)

    def one(i, carry):
        return body(pl.multiple_of(first + i * step, SUB), step, carry)

    return lax.fori_loop(0, rows // step, one, 0 if init is None else init)


def beside(parts):
    lane = lax.broadcasted_iota(jnp.int32, parts[0].shape, 1)
    ahead = [pltpu.roll(v, 1, 1) for v in parts]
    after = [pltpu.roll(v, LANES - 1, 1) for v in parts]
    out = []
    for h in range(len(parts)):
        before = ahead[h - 1] if h else jnp.zeros_like(parts[0])
        behind = after[h + 1] if h + 1 < len(parts) else jnp.zeros_like(parts[0])
        out.append(
            jnp.where(lane == 0, before, ahead[h])
            + jnp.where(lane == LANES - 1, behind, after[h])
        )
    return out


def around(field, at, rows, groups):
    mid = [field[h, pl.ds(at + SUB, rows), :] for h in range(groups)]
    side = beside(mid)
    total = [
        side[h] + field[h, pl.ds(at + SUB - 1, rows), :] + field[h, pl.ds(at + SUB + 1, rows), :]
        for h in range(groups)
    ]
    return mid, total


def gather_taps(taps, field, at, rows, groups):
    acc = [None] * groups
    for j, k in enumerate(TAPS):
        tap = taps[j, pl.ds(at + SUB, rows), :]
        for h in range(groups):
            term = tap * field[h, pl.ds(at + SUB + k, rows), :]
            acc[h] = term if acc[h] is None else acc[h] + term
    return acc


def return_taps(taps, field, at, rows, groups, acc):
    acc = list(acc)
    for j, k in enumerate(TAPS):
        tap = taps[j, pl.ds(at + SUB - k, rows), :]
        for h in range(groups):
            acc[h] = acc[h] + tap * field[h, pl.ds(at + SUB - k, rows), :]
    return acc


def before_kernel(rows, groups, plan, b, cr, prev, nxt, *refs):
    pieces, (taps, bs, crs, proj, base, scratch, share, offs) = refs[: len(plan)], refs[len(plan) :]
    frame = rows + 2 * HALO
    edge = jnp.zeros((SUB, LANES), jnp.float32)
    for h in range(groups):
        lanes = slice(h * LANES, (h + 1) * LANES)
        bs[h, 0:SUB, :] = edge
        bs[h, SUB : SUB + HALO, :] = prev[0:HALO, lanes]
        bs[h, SUB + HALO : SUB + HALO + rows, :] = b[:, lanes]
        bs[h, SUB + HALO + rows : SUB + frame, :] = nxt[0:HALO, lanes]
        bs[h, SUB + frame :, :] = edge
        for lo, hi in ((0, HALO - SPAN), (frame - HALO + SPAN, frame)):
            crs[h, lo:hi, :] = jnp.zeros((hi - lo, LANES), jnp.float32)
        crs[h, HALO - SPAN : HALO, :] = prev[HALO : HALO + SPAN, lanes]
        crs[h, HALO : HALO + rows, :] = cr[:, lanes]
        crs[h, HALO + rows : HALO + rows + SPAN, :] = nxt[HALO : HALO + SPAN, lanes]
        for field in (proj, scratch):
            field[h, 0:SUB, :] = edge
            field[h, SUB + frame :, :] = edge
    for piece, (first, length, row) in zip(pieces, plan, strict=True):
        width = groups * LANES
        lines = -(-length // width)
        for target, line in ((share, row), (offs, row + lines)):
            for start in range(0, length, LANES):
                count = min(LANES, length - start)
                r, c = line + start // width, start % width
                square = jnp.broadcast_to(piece[r : r + 1, c : c + LANES], (LANES, LANES)).T
                target[first + start : first + start + count, :] = square[:count]
    for j in range(len(TAPS)):
        taps[j, 0:SUB, :] = edge
        taps[j, SUB + frame :, :] = edge

    def fill(at, step, carry):
        part = share[pl.ds(at, step), :]
        rest = 1.0 - part
        off = offs[pl.ds(at, step), :]
        for j, k in enumerate(TAPS):
            taps[j, pl.ds(at + SUB, step), :] = jnp.where(
                off == k, part, jnp.where(off == k - 1, rest, 0.0)
            )
        return carry

    for_chunks(0, frame, fill)

    def project(at, step, carry):
        acc = gather_taps(taps, bs, at, step, groups)
        for h in range(groups):
            proj[h, pl.ds(at + SUB, step), :] = acc[h]
        return carry

    for_chunks(0, frame, project)

    def neighbours(at, step, carry):
        _, total = around(proj, at, step, groups)
        for h in range(groups):
            scratch[h, pl.ds(at + SUB, step), :] = -0.25 * total[h]
        return carry

    for_chunks(0, frame, neighbours)

    def start(at, step, carry):
        mid, total = around(bs, at, step, groups)
        acc = [crs[h, pl.ds(at, step), :] * mid[h] - 0.25 * total[h] for h in range(groups)]
        acc = return_taps(taps, scratch, at, step, groups, acc)
        for h in range(groups):
            base[h, pl.ds(at, step), :] = acc[h]
        return carry

    for_chunks(0, frame, start)


def apply_kernel(rows, groups, devices, plan, taps, bs, crs, proj, base, *refs):
    pieces = refs[: len(plan)]
    image, second, sums, resp, cs, proj_two = refs[len(plan) :]
    frame = rows + 2 * HALO
    edge = jnp.zeros((SUB, LANES), jnp.float32)
    for h in range(groups):
        lanes = slice(h * LANES, (h + 1) * LANES)
        for piece, (first, length, _) in zip(pieces, plan, strict=True):
            cs[h, first : first + length, :] = piece[:, lanes]
        for field in (image, resp, proj_two):
            field[h, 0:SUB, :] = edge
            field[h, SUB + frame :, :] = edge

    def scale(at, step, carry):
        for h in range(groups):
            resp[h, pl.ds(at + SUB, step), :] = (
                cs[h, pl.ds(at, step), :] * proj[h, pl.ds(at + SUB, step), :]
            )
        return carry

    for_chunks(0, frame, scale)

    def first(at, step, carry):
        acc = [base[h, pl.ds(at, step), :] for h in range(groups)]
        acc = return_taps(taps, resp, at, step, groups, acc)
        for h in range(groups):
            image[h, pl.ds(at + SUB, step), :] = acc[h]
        return carry

    for_chunks(0, frame, first)

    def project(at, step, carry):
        acc = gather_taps(taps, image, at, step, groups)
        for h in range(groups):
            proj_two[h, pl.ds(at + SUB, step), :] = acc[h]
        return carry

    for_chunks(0, frame, project)

    def respond(at, step, carry):
        mid, total = around(proj_two, at, step, groups)
        for h in range(groups):
            resp[h, pl.ds(at + SUB, step), :] = (
                cs[h, pl.ds(at, step), :] * mid[h] - 0.25 * total[h]
            )
        return carry

    for_chunks(0, frame, respond)

    def last(at, step, carry):
        mid, total = around(image, at, step, groups)
        acc = [crs[h, pl.ds(at, step), :] * mid[h] - 0.25 * total[h] for h in range(groups)]
        acc = return_taps(taps, resp, at, step, groups, acc)
        carry = list(carry)
        for h in range(groups):
            second[h, pl.ds(at - HALO, step), :] = acc[h]
            right = bs[h, pl.ds(at + SUB, step), :]
            pairs = ((right, mid[h]), (right, acc[h]), (mid[h], mid[h]), (mid[h], acc[h]), (acc[h], acc[h]))
            for j, (u, v) in enumerate(pairs):
                carry[j] = carry[j] + jnp.sum((u * v).reshape(step // SUB, SUB, LANES), axis=0)
        return tuple(carry)

    totals = for_chunks(HALO, rows, last, tuple(jnp.zeros((SUB, LANES), jnp.float32) for _ in range(5)))
    lane = lax.broadcasted_iota(jnp.int32, (SUB, LANES), 1)
    line = jnp.zeros((SUB, LANES), jnp.float32)
    for j, total in enumerate(totals):
        line = jnp.where(lane == j, jnp.sum(total), line)
    sums[...] = jnp.broadcast_to(line[0:1], (devices, LANES))


def finish_kernel(rows, groups, parts, bs, image, second, solution_out, residual_out, sol, res, sems):
    total = jnp.sum(parts[...], axis=0, keepdims=True)
    b_p, b_q, p_p, p_q, q_q = (total[:, j : j + 1] for j in range(5))
    det = p_p * q_q - p_q * p_q
    y1 = (q_q * b_p - p_q * b_q) / det
    y2 = (p_p * b_q - p_q * b_p) / det
    step = chunk_of(rows, 128)
    copies = []
    for i in range(rows // step):
        at = i * step
        one = jnp.broadcast_to(y1, (step, LANES))
        two = jnp.broadcast_to(y2, (step, LANES))
        for h in range(groups):
            lanes = slice(h * LANES, (h + 1) * LANES)
            b = bs[h, at + SUB + HALO : at + SUB + HALO + step, :]
            p = image[h, at + SUB + HALO : at + SUB + HALO + step, :]
            q = second[h, at : at + step, :]
            sol[at : at + step, lanes] = one * b + two * p
            res[at : at + step, lanes] = b - one * p - two * q
        for j, (src, dst) in enumerate(((sol, solution_out), (res, residual_out))):
            copy = pltpu.make_async_copy(
                src.at[pl.ds(at, step)], dst.at[pl.ds(at, step)], sems.at[i, j]
            )
            copy.start()
            copies.append(copy)
    for copy in copies:
        copy.wait()


def local(right_side, coef_rotor, coef_stator, mortar_rows, mortar_weight):
    rows, cols = right_side.shape
    groups = cols // LANES
    count = lax.axis_size("circ")
    devices = count * lax.axis_size("radax")
    total_rows = rows * count
    frame = rows + 2 * HALO
    whole, remainder = divmod(SLIDE, rows)
    assert cols == W and rows % SUB == 0 and remainder % SUB == 0
    assert HALO <= remainder <= rows - HALO

    stator = lax.axis_index("circ") * rows + jnp.arange(rows, dtype=jnp.int32)
    offset = jnp.mod(mortar_rows - stator - SLIDE + total_rows // 2, total_rows) - total_rows // 2
    offset = offset.astype(jnp.float32)
    routes = [(whole + 1, rows - remainder - HALO, rows), (whole, 0, rows - remainder + HALO)]
    coefs = [shifted(coef_stator[lo:hi], by) for by, lo, hi in routes]

    mail = {}

    def post(by, block):
        blocks = mail.setdefault(by % count, [])
        at = sum(x.shape[0] for x in blocks)
        blocks.append(jnp.pad(block, ((0, up8(block.shape[0]) - block.shape[0]), (0, 0))))
        return by % count, at, block.shape[0]

    def in_lines(vector):
        lines = -(-vector.shape[0] // cols)
        return jnp.pad(vector, (0, lines * cols - vector.shape[0])).reshape(lines, cols)

    tags = [
        post(1, jnp.concatenate([right_side[rows - HALO :], coef_rotor[rows - SPAN :]])),
        post(-1, jnp.concatenate([right_side[:HALO], coef_rotor[:SPAN]])),
    ]
    for by, lo, hi in routes:
        tags.append(post(by, jnp.concatenate([in_lines(mortar_weight[lo:hi]), in_lines(offset[lo:hi])])))
    arrived = {by: shifted(jnp.concatenate(blocks), by) for by, blocks in mail.items()}
    prev, nxt, *pieces = [arrived[by][at : at + up8(size)] for by, at, size in tags]

    plan, first = [], 0
    for _, lo, hi in routes:
        plan.append((first, hi - lo, 0))
        first += hi - lo

    def vmem(*shape):
        return pltpu.VMEM(shape, jnp.float32)

    held = rows + 2 * HALO + 2 * SUB
    taps, bs, crs, proj, base = pl.pallas_call(
        functools.partial(before_kernel, rows, groups, plan),
        out_shape=[
            vmem(len(TAPS), held, LANES),
            vmem(groups, held, LANES),
            vmem(groups, frame, LANES),
            vmem(groups, held, LANES),
            vmem(groups, frame, LANES),
        ],
        in_specs=[VMEM] * (4 + len(pieces)),
        out_specs=[VMEM] * 5,
        scratch_shapes=[vmem(groups, held, LANES), vmem(frame, LANES), vmem(frame, LANES)],
        compiler_params=PARAMS,
        name="before",
    )(right_side, coef_rotor, prev, nxt, *pieces)

    image, second, sums = pl.pallas_call(
        functools.partial(apply_kernel, rows, groups, devices, plan),
        out_shape=[
            vmem(groups, held, LANES),
            vmem(groups, rows, LANES),
            vmem(devices, LANES),
        ],
        in_specs=[VMEM] * (5 + len(coefs)),
        out_specs=[VMEM] * 3,
        scratch_shapes=[vmem(groups, held, LANES), vmem(groups, frame, LANES), vmem(groups, held, LANES)],
        compiler_params=PARAMS,
        name="apply",
    )(taps, bs, crs, proj, base, *coefs)

    parts = lax.all_to_all(sums, ("circ", "radax"), 0, 0, tiled=True)

    step = chunk_of(rows, 128)
    return pl.pallas_call(
        functools.partial(finish_kernel, rows, groups),
        out_shape=[jax.ShapeDtypeStruct((rows, cols), jnp.float32)] * 2,
        in_specs=[VMEM] * 4,
        out_specs=[pl.BlockSpec(memory_space=pl.ANY)] * 2,
        scratch_shapes=[
            vmem(rows, cols),
            vmem(rows, cols),
            pltpu.SemaphoreType.DMA((rows // step, 2)),
        ],
        compiler_params=PARAMS,
        name="finish",
    )(parts, bs, image, second)


def solution(mesh):
    return jax.shard_map(
        local,
        mesh=mesh,
        in_specs=(P("circ", "radax"), P("circ", "radax"), P("circ", "radax"), P("circ"), P("circ")),
        out_specs=(P("circ", "radax"), P("circ", "radax")),
        check_vma=False,
    )
```

```python
import functools

import jax
import jax.numpy as jnp
import numpy as np
from jax import lax
from jax.experimental import pallas as pl
from jax.experimental.pallas import tpu as pltpu
from jax.sharding import PartitionSpec as P

W = 256
REACH = 3
SLIDE = 1280

LANES = 128
SUB = 8
SPAN = 2 * (REACH + 1)
HALO = 2 * SPAN
TAPS = range(-REACH, REACH + 2)
CHUNK = 64
LATER = (1, 3)
VMEM = pl.BlockSpec(memory_space=pltpu.VMEM)
PARAMS = pltpu.CompilerParams(vmem_limit_bytes=40 << 20)


def up8(count):
    return -(-count // SUB) * SUB


def vmem(*shape):
    return pltpu.VMEM(shape, jnp.float32)


def shifted(block, distance):
    count = lax.axis_size("circ")
    route = [((i - distance) % count, i) for i in range(count)]
    return lax.ppermute(block, "circ", route)


def near(mask, low, high):
    out = np.ones_like(mask)
    for k in range(low, high + 1):
        moved = np.zeros_like(mask)
        moved[max(0, -k) : len(mask) - max(0, k)] = mask[max(0, k) : len(mask) - max(0, -k)]
        out &= moved
    return out


def spread(mask, low, high):
    return ~near(~mask, -high, -low)


STAGES = ("proj", "resp", "image", "proj_two", "resp_two", "second")


def reachable(own, trace, coef, tap):
    proj = tap & near(trace, TAPS[0], TAPS[-1])
    resp = coef & near(proj, -1, 1)
    image = trace & near(trace, -1, 1) & near(resp & tap, -TAPS[-1], -TAPS[0])
    proj_two = tap & near(image, TAPS[0], TAPS[-1])
    resp_two = coef & near(proj_two, -1, 1)
    second = own & near(image, -1, 1) & near(resp_two & tap, -TAPS[-1], -TAPS[0])
    return dict(zip(STAGES, (proj, resp, image, proj_two, resp_two, second), strict=True))


def needed(own):
    resp_two = spread(own, -TAPS[-1], -TAPS[0])
    proj_two = spread(resp_two, -1, 1)
    image = spread(own, -1, 1) | spread(proj_two, TAPS[0], TAPS[-1])
    resp = spread(image, -TAPS[-1], -TAPS[0])
    proj = spread(resp, -1, 1)
    return dict(zip(STAGES, (proj, resp, image, proj_two, resp_two, own), strict=True))


def spans(mask, whole):
    tiles = mask.reshape(-1, SUB)
    tiles = tiles.all(1) if whole else tiles.any(1)
    edges = np.flatnonzero(np.diff(np.concatenate([[0], tiles.astype(np.int8), [0]])))
    return [(int(a) * SUB, int(b) * SUB) for a, b in zip(edges[::2], edges[1::2], strict=True)]


def for_chunks(ranges, body, carry=None):
    for first, last in ranges:
        for at in range(first, last, CHUNK):
            carry = body(at, min(CHUNK, last - at), carry)
    return carry


def beside(parts):
    lane = lax.broadcasted_iota(jnp.int32, parts[0].shape, 1)
    ahead = [pltpu.roll(v, 1, 1) for v in parts]
    after = [pltpu.roll(v, LANES - 1, 1) for v in parts]
    out = []
    for h in range(len(parts)):
        before = ahead[h - 1] if h else jnp.zeros_like(parts[0])
        behind = after[h + 1] if h + 1 < len(parts) else jnp.zeros_like(parts[0])
        out.append(
            jnp.where(lane == 0, before, ahead[h])
            + jnp.where(lane == LANES - 1, behind, after[h])
        )
    return out


def around(field, at, step):
    groups = field.shape[0]
    at += SUB
    mid = [field[h, at : at + step, :] for h in range(groups)]
    side = beside(mid)
    total = [
        side[h] + field[h, at - 1 : at - 1 + step, :] + field[h, at + 1 : at + 1 + step, :]
        for h in range(groups)
    ]
    return mid, total


def project(taps, field, at, step):
    acc = [None] * field.shape[0]
    at += SUB
    for j, k in enumerate(TAPS):
        tap = taps[j, at : at + step, :]
        for h in range(len(acc)):
            term = tap * field[h, at + k : at + k + step, :]
            acc[h] = term if acc[h] is None else acc[h] + term
    return acc


def give_back(taps, field, at, step, acc):
    acc = list(acc)
    at += SUB
    for j, k in enumerate(TAPS):
        tap = taps[j, at - k : at - k + step, :]
        for h in range(len(acc)):
            acc[h] = acc[h] + tap * field[h, at - k : at - k + step, :]
    return acc


def pack_kernel(rows, total_rows, messages, b, cr, cs, mortar, weight, *refs):
    outs, (mortar_here, weight_here, lines, sems) = refs[: len(messages)], refs[len(messages) :]
    sources = {"trace": b, "rotor": cr, "stator": cs}
    small = [
        pltpu.make_async_copy(mortar, mortar_here, sems.at[-1 + sems.shape[0]]),
        pltpu.make_async_copy(weight, weight_here, sems.at[-2 + sems.shape[0]]),
    ]
    for copy in small:
        copy.start()
    copies = []
    for out, (_, parts) in zip(outs, messages, strict=True):
        for kind, row, what in parts:
            if kind == "lines":
                continue
            for source, low, size, skip in what:
                copy = pltpu.make_async_copy(
                    sources[source].at[pl.ds(low, size)], out.at[pl.ds(row + skip, size)], sems.at[len(copies)]
                )
                copy.start()
                copies.append(copy)
    for copy in small:
        copy.wait()
    count = rows // LANES
    shape = (count, LANES)
    facing = lax.rem(lax.axis_index("circ") * rows + SLIDE, total_rows)
    facing = (
        facing
        + lax.broadcasted_iota(jnp.int32, shape, 0) * LANES
        + lax.broadcasted_iota(jnp.int32, shape, 1)
    )
    offset = mortar_here[...] - jnp.where(facing >= total_rows, facing - total_rows, facing)
    offset = jnp.where(offset > total_rows // 2, offset - total_rows, offset)
    offset = jnp.where(offset < -(total_rows // 2), offset + total_rows, offset)
    lines[:, 0:LANES] = weight_here[...]
    lines[:, LANES : 2 * LANES] = offset.astype(jnp.float32)
    for copy in copies:
        copy.wait()
    for out, (_, parts) in zip(outs, messages, strict=True):
        for kind, row, _ in parts:
            if kind == "lines":
                out[row : row + count, :] = lines[...]


STATE = ("trace", "coef", "taps", *STAGES, "sums")


def step_kernel(rows, opening, closing, work, fills, coefs, count, *refs):
    refs = list(refs)
    mail = refs[:count]
    refs = refs[count:]
    if work["starts"]:
        own, own_coef = refs[:2]
        refs = refs[2:]
    else:
        refs = refs[len(STATE) :]
    state = dict(zip(STATE, refs, strict=False))
    rest = refs[len(STATE) :]
    trace, coef, taps = state["trace"], state["coef"], state["taps"]
    groups = trace.shape[0]
    frame = rows + 2 * HALO

    for h in range(groups):
        lanes = slice(h * LANES, (h + 1) * LANES)
        if work["starts"]:
            trace[h, SUB + HALO : SUB + HALO + rows, :] = own[:, lanes]
            coef[h, HALO : HALO + rows, :] = own_coef[:, lanes]
        for edge, m, row in opening:
            at = 0 if edge == "head" else HALO + rows
            trace[h, SUB + at : SUB + at + HALO, :] = mail[m][row : row + HALO, lanes]
            at = HALO - SPAN if edge == "head" else HALO + rows
            coef[h, at : at + SPAN, :] = mail[m][row + HALO : row + HALO + SPAN, lanes]

    share, offs = rest[-2:]
    for m, row, low, high, first in fills:
        for line in range(low // LANES, -(-high // LANES)):
            a, b = max(low, line * LANES), min(high, (line + 1) * LANES)
            at, skip, size = first + a - low, a - line * LANES, b - a
            for target, lane in ((share, 0), (offs, LANES)):
                values = mail[m][row + line : row + line + 1, lane : lane + LANES]
                square = jnp.broadcast_to(values, (LANES, LANES)).T
                target[at : at + size, :] = square[skip : skip + size]

        def fill(at, step, carry):
            part, off = share[at : at + step, :], offs[at : at + step, :]
            for j, k in enumerate(TAPS):
                taps[j, at + SUB : at + SUB + step, :] = jnp.where(
                    off == k, part, jnp.where(off == k - 1, 1.0 - part, 0.0)
                )
            return carry

        for_chunks([(first, first + high - low)], fill)

    def plain_project(source, target):
        def body(at, step, carry):
            for h, value in enumerate(project(taps, source, at, step)):
                target[h, at + SUB : at + SUB + step, :] = value
            return carry

        return body

    def respond(source, target, ranges):
        for m, row, first, end in coefs:
            def body(at, step, carry, m=m, row=row, first=first):
                mid, total = around(source, at, step)
                for h in range(groups):
                    scale = mail[m][row + at - first : row + at - first + step, h * LANES : (h + 1) * LANES]
                    target[h, at + SUB : at + SUB + step, :] = scale * mid[h] - 0.25 * total[h]
                return carry

            for_chunks([(max(a, first), min(b, end)) for a, b in ranges if max(a, first) < min(b, end)], body)

    def apply(source, response, at, step):
        mid, total = around(source, at, step)
        acc = [coef[h, at : at + step, :] * mid[h] - 0.25 * total[h] for h in range(groups)]
        return mid, give_back(taps, response, at, step, acc)

    def first_image(at, step, carry):
        for h, value in enumerate(apply(trace, state["resp"], at, step)[1]):
            state["image"][h, at + SUB : at + SUB + step, :] = value
        return carry

    def second_image(at, step, carry):
        mid, acc = apply(state["image"], state["resp_two"], at, step)
        carry = list(carry)
        for h in range(groups):
            state["second"][h, at - HALO : at - HALO + step, :] = acc[h]
            right = trace[h, at + SUB : at + SUB + step, :]
            pairs = ((right, mid[h]), (right, acc[h]), (mid[h], mid[h]), (mid[h], acc[h]), (acc[h], acc[h]))
            for j, (u, v) in enumerate(pairs):
                carry[j] = carry[j] + jnp.sum((u * v).reshape(step // SUB, SUB, LANES), axis=0)
        return carry

    for_chunks(work["proj"], plain_project(trace, state["proj"]))
    respond(state["proj"], state["resp"], work["resp"])
    for_chunks(work["image"], first_image)
    for_chunks(work["proj_two"], plain_project(state["image"], state["proj_two"]))
    respond(state["proj_two"], state["resp_two"], work["resp_two"])
    if work["starts"]:
        totals = [jnp.zeros((SUB, LANES), jnp.float32)] * 5
    else:
        totals = [state["sums"][j] for j in range(5)]
    totals = for_chunks(work["second"], second_image, totals)
    if closing:
        lane = lax.broadcasted_iota(jnp.int32, (SUB, LANES), 1)
        line = jnp.zeros((SUB, LANES), jnp.float32)
        for j, total in enumerate(totals):
            line = jnp.where(lane == j, jnp.sum(total), line)
        rest[0][...] = jnp.broadcast_to(line[0:1], rest[0].shape)
    else:
        for j, total in enumerate(totals):
            state["sums"][j] = total
    del frame


def finish_kernel(rows, groups, parts, trace, image, second, solution_out, residual_out, sol, res, sems):
    total = jnp.sum(parts[...], axis=0, keepdims=True)
    b_p, b_q, p_p, p_q, q_q = (total[:, j : j + 1] for j in range(5))
    det = p_p * q_q - p_q * p_q
    y1 = (q_q * b_p - p_q * b_q) / det
    y2 = (p_p * b_q - p_q * b_p) / det
    step = rows // 4
    copies = []
    for i in range(rows // step):
        at = i * step
        one = jnp.broadcast_to(y1, (step, LANES))
        two = jnp.broadcast_to(y2, (step, LANES))
        for h in range(groups):
            lanes = slice(h * LANES, (h + 1) * LANES)
            b = trace[h, at + SUB + HALO : at + SUB + HALO + step, :]
            p = image[h, at + SUB + HALO : at + SUB + HALO + step, :]
            q = second[h, at : at + step, :]
            sol[at : at + step, lanes] = one * b + two * p
            res[at : at + step, lanes] = b - one * p - two * q
        for j, (src, dst) in enumerate(((sol, solution_out), (res, residual_out))):
            copy = pltpu.make_async_copy(
                src.at[pl.ds(at, step)], dst.at[pl.ds(at, step)], sems.at[i, j]
            )
            copy.start()
            copies.append(copy)
    for copy in copies:
        copy.wait()


def local(right_side, coef_rotor, coef_stator, mortar_rows, mortar_weight):
    rows, cols = right_side.shape
    groups = cols // LANES
    count = lax.axis_size("circ")
    devices = count * lax.axis_size("radax")
    total_rows = rows * count
    frame = rows + 2 * HALO
    held = frame + 2 * SUB
    whole, remainder = divmod(SLIDE, rows)
    assert cols == W and rows % (4 * SUB) == 0 and remainder % SUB == 0
    assert HALO <= remainder <= rows - HALO

    assert rows % LANES == 0

    cut = remainder + HALO
    count_lines = rows // LANES
    spare = HALO - SPAN - REACH - 1
    assert count_lines <= spare
    later = frame - up8((frame - cut) * LATER[0] // LATER[1])
    below, above = whole + 1, whole

    def stator_rows(first, last, low):
        return ("coef", [("stator", first - low, last - first, 0)], first, last)

    low_below, low_above = cut - rows, cut
    edge = ("tail", [("trace", 0, HALO, 0), ("rotor", 0, SPAN, HALO)])
    start = ("head", [("trace", rows - HALO, HALO, 0), ("rotor", rows - SPAN, SPAN, HALO)])
    sent = [
        (below, [stator_rows(0, cut, low_below), ("lines", 0, rows - cut, rows, 0)]),
        (above, [stator_rows(cut, later, low_above), ("lines", None, 0, rows - cut + 2 * HALO, cut)]),
        (above, [stator_rows(later, frame, low_above)]),
        (1, [start]),
    ]
    if (below + 1) % count == 0:
        sent[0][1].append(edge)
    else:
        sent.append((-1, [edge]))
    messages, holds, heights = [], [], []
    for by, parts in sent:
        row, laid = 0, []
        for kind, what, *_ in parts:
            if kind == "lines" and what is not None:
                laid.append((kind, what, None))
                continue
            laid.append((kind, row, what))
            row += up8(count_lines if kind == "lines" else sum(size for _, _, size, _ in what))
        messages.append((by, laid))
        holds.append([(kind, at, rest) for (kind, at, _), (_, _, *rest) in zip(laid, parts, strict=True)])
        heights.append(row)
    copies = sum(len(what) for _, laid in messages for kind, _, what in laid if kind != "lines")
    packed = pl.pallas_call(
        functools.partial(pack_kernel, rows, total_rows, messages),
        out_shape=[vmem(height, cols) for height in heights],
        in_specs=[pl.BlockSpec(memory_space=pltpu.HBM)] * 5,
        out_specs=[VMEM] * len(messages),
        scratch_shapes=[
            pltpu.VMEM((count_lines, LANES), jnp.int32),
            vmem(count_lines, LANES),
            vmem(count_lines, cols),
            pltpu.SemaphoreType.DMA((copies + 2,)),
        ],
        compiler_params=PARAMS,
        name="pack",
    )(
        *(
            pltpu.with_memory_space_constraint(x, pltpu.HBM)
            for x in (
                right_side,
                coef_rotor,
                coef_stator,
                mortar_rows.reshape(count_lines, LANES),
                mortar_weight.reshape(count_lines, LANES),
            )
        )
    )
    arrived = [shifted(block, by) for block, (by, _) in zip(packed, messages, strict=True)]

    own = np.zeros(frame, bool)
    own[HALO : HALO + rows] = True
    known = {"trace": own.copy(), "coef": np.zeros(frame, bool), "taps": np.zeros(frame, bool)}
    done = {name: np.zeros(frame, bool) for name in STAGES}
    want = needed(own)
    coefs = []
    shapes = {name: vmem(groups, held, LANES) for name in STATE}
    shapes["coef"] = vmem(groups, frame, LANES)
    shapes["taps"] = vmem(len(TAPS), held, LANES)
    shapes["second"] = vmem(groups, rows, LANES)
    shapes["sums"] = vmem(5, SUB, LANES)

    steps = [[0], [1], list(range(2, len(sent)))]
    state, taken = None, []
    for number, batch in enumerate(steps):
        opening, fills = [], []
        for m in batch:
            taken.append(m)
            for kind, at, what in holds[m]:
                if kind in ("head", "tail"):
                    opening.append((kind, len(taken) - 1, at))
                    known["trace"][slice(0, HALO) if kind == "head" else slice(frame - HALO, frame)] = True
                elif kind == "lines":
                    low, high, first = what
                    fills.append((len(taken) - 1, at, low, high, first))
                    known["taps"][first : first + high - low] = True
                else:
                    first, last = what
                    coefs.append((len(taken) - 1, at, first, last))
                    known["coef"][max(first, spare) : last] = True
        can = reachable(own, known["trace"], known["coef"], known["taps"])
        work = {"starts": number == 0}
        for name in STAGES:
            whole_tiles = name == "second"
            work[name] = spans(can[name] & want[name] & ~done[name], whole_tiles)
            if whole_tiles:
                for a, b in work[name]:
                    done[name][a:b] = True
            else:
                done[name] |= can[name] & want[name]
        closing = number == len(steps) - 1
        out_shape = [shapes[name] for name in STATE] + [vmem(devices, LANES)] * closing
        inputs = [arrived[m] for m in taken]
        state = pl.pallas_call(
            functools.partial(
                step_kernel, rows, opening, closing, work, fills, list(coefs), len(taken)
            ),
            out_shape=out_shape,
            in_specs=[VMEM] * (len(taken) + (2 if number == 0 else len(STATE))),
            out_specs=[VMEM] * len(out_shape),
            scratch_shapes=[vmem(frame, LANES)] * 2,
            input_output_aliases={} if number == 0 else {len(taken) + i: i for i in range(len(STATE))},
            compiler_params=PARAMS,
            name=f"step{number}",
        )(*inputs, *([right_side, coef_rotor] if number == 0 else state))
    *state, line = state
    assert done["second"][HALO : HALO + rows].all()
    state = dict(zip(STATE, state, strict=True))

    parts = lax.all_to_all(line, ("circ", "radax"), 0, 0, tiled=True)

    return pl.pallas_call(
        functools.partial(finish_kernel, rows, groups),
        out_shape=[jax.ShapeDtypeStruct((rows, cols), jnp.float32)] * 2,
        in_specs=[VMEM] * 4,
        out_specs=[pl.BlockSpec(memory_space=pl.ANY)] * 2,
        scratch_shapes=[
            vmem(rows, cols),
            vmem(rows, cols),
            pltpu.SemaphoreType.DMA((4, 2)),
        ],
        compiler_params=PARAMS,
        name="finish",
    )(parts, state["trace"], state["image"], state["second"])


def solution(mesh):
    return jax.shard_map(
        local,
        mesh=mesh,
        in_specs=(P("circ", "radax"), P("circ", "radax"), P("circ", "radax"), P("circ"), P("circ")),
        out_specs=(P("circ", "radax"), P("circ", "radax")),
        check_vma=False,
    )
```

```python
import functools

import jax
import jax.numpy as jnp
import numpy as np
from jax import lax
from jax.experimental import pallas as pl
from jax.experimental.pallas import tpu as pltpu
from jax.sharding import PartitionSpec as P

W = 256
REACH = 3
SLIDE = 1280

LANES = 128
SUB = 8
SPAN = 2 * (REACH + 1)
HALO = 2 * SPAN
TAPS = range(-REACH, REACH + 2)
CHUNK = 64
WRITES = 4
LATER = (1, 4), (1, 2)
VMEM = pl.BlockSpec(memory_space=pltpu.VMEM)
PARAMS = pltpu.CompilerParams(vmem_limit_bytes=40 << 20)


def up8(count):
    return -(-count // SUB) * SUB


def vmem(*shape):
    return pltpu.VMEM(shape, jnp.float32)


def shifted(block, distance):
    count = lax.axis_size("circ")
    route = [((i - distance) % count, i) for i in range(count)]
    return lax.ppermute(block, "circ", route)


def near(mask, low, high):
    out = np.ones_like(mask)
    for k in range(low, high + 1):
        moved = np.zeros_like(mask)
        moved[max(0, -k) : len(mask) - max(0, k)] = mask[max(0, k) : len(mask) - max(0, -k)]
        out &= moved
    return out


def spread(mask, low, high):
    return ~near(~mask, -high, -low)


STAGES = ("proj", "resp", "image", "proj_two", "resp_two", "second")


def reachable(own, trace, coef, tap):
    proj = tap & near(trace, TAPS[0], TAPS[-1])
    resp = coef & near(proj, -1, 1)
    image = trace & near(trace, -1, 1) & near(resp & tap, -TAPS[-1], -TAPS[0])
    proj_two = tap & near(image, TAPS[0], TAPS[-1])
    resp_two = coef & near(proj_two, -1, 1)
    second = own & near(image, -1, 1) & near(resp_two & tap, -TAPS[-1], -TAPS[0])
    return dict(zip(STAGES, (proj, resp, image, proj_two, resp_two, second), strict=True))


def needed(own):
    resp_two = spread(own, -TAPS[-1], -TAPS[0])
    proj_two = spread(resp_two, -1, 1)
    image = spread(own, -1, 1) | spread(proj_two, TAPS[0], TAPS[-1])
    resp = spread(image, -TAPS[-1], -TAPS[0])
    proj = spread(resp, -1, 1)
    return dict(zip(STAGES, (proj, resp, image, proj_two, resp_two, own), strict=True))


def spans(mask, whole):
    tiles = mask.reshape(-1, SUB)
    tiles = tiles.all(1) if whole else tiles.any(1)
    edges = np.flatnonzero(np.diff(np.concatenate([[0], tiles.astype(np.int8), [0]])))
    return [(int(a) * SUB, int(b) * SUB) for a, b in zip(edges[::2], edges[1::2], strict=True)]


def for_chunks(ranges, body, carry=None):
    for first, last in ranges:
        for at in range(first, last, CHUNK):
            carry = body(at, min(CHUNK, last - at), carry)
    return carry


def beside(parts):
    lane = lax.broadcasted_iota(jnp.int32, parts[0].shape, 1)
    ahead = [pltpu.roll(v, 1, 1) for v in parts]
    after = [pltpu.roll(v, LANES - 1, 1) for v in parts]
    out = []
    for h in range(len(parts)):
        before = ahead[h - 1] if h else jnp.zeros_like(parts[0])
        behind = after[h + 1] if h + 1 < len(parts) else jnp.zeros_like(parts[0])
        out.append(
            jnp.where(lane == 0, before, ahead[h])
            + jnp.where(lane == LANES - 1, behind, after[h])
        )
    return out


def around(field, at, step):
    groups = field.shape[0]
    at += SUB
    mid = [field[h, at : at + step, :] for h in range(groups)]
    side = beside(mid)
    total = [
        side[h] + field[h, at - 1 : at - 1 + step, :] + field[h, at + 1 : at + 1 + step, :]
        for h in range(groups)
    ]
    return mid, total


def project(taps, field, at, step):
    acc = [None] * field.shape[0]
    at += SUB
    for j, k in enumerate(TAPS):
        tap = taps[j, at : at + step, :]
        for h in range(len(acc)):
            term = tap * field[h, at + k : at + k + step, :]
            acc[h] = term if acc[h] is None else acc[h] + term
    return acc


def give_back(taps, field, at, step, acc):
    acc = list(acc)
    at += SUB
    for j, k in enumerate(TAPS):
        tap = taps[j, at - k : at - k + step, :]
        for h in range(len(acc)):
            acc[h] = acc[h] + tap * field[h, at - k : at - k + step, :]
    return acc


def pack_kernel(rows, total_rows, messages, b, cr, cs, mortar, weight, *refs):
    outs, (mortar_here, weight_here, lines, sems) = refs[: len(messages)], refs[len(messages) :]
    sources = {"trace": b, "rotor": cr, "stator": cs}
    small = [
        pltpu.make_async_copy(mortar, mortar_here, sems.at[-1 + sems.shape[0]]),
        pltpu.make_async_copy(weight, weight_here, sems.at[-2 + sems.shape[0]]),
    ]
    for copy in small:
        copy.start()
    copies = []
    for out, (_, parts) in zip(outs, messages, strict=True):
        for kind, row, what in parts:
            if kind == "lines":
                continue
            for source, low, size, skip in what:
                copy = pltpu.make_async_copy(
                    sources[source].at[pl.ds(low, size)], out.at[pl.ds(row + skip, size)], sems.at[len(copies)]
                )
                copy.start()
                copies.append(copy)
    for copy in small:
        copy.wait()
    count = rows // LANES
    shape = (count, LANES)
    facing = lax.rem(lax.axis_index("circ") * rows + SLIDE, total_rows)
    facing = (
        facing
        + lax.broadcasted_iota(jnp.int32, shape, 0) * LANES
        + lax.broadcasted_iota(jnp.int32, shape, 1)
    )
    offset = mortar_here[...] - jnp.where(facing >= total_rows, facing - total_rows, facing)
    offset = jnp.where(offset > total_rows // 2, offset - total_rows, offset)
    offset = jnp.where(offset < -(total_rows // 2), offset + total_rows, offset)
    lines[:, 0:LANES] = weight_here[...]
    lines[:, LANES : 2 * LANES] = offset.astype(jnp.float32)
    for copy in copies:
        copy.wait()
    for out, (_, parts) in zip(outs, messages, strict=True):
        for kind, row, _ in parts:
            if kind == "lines":
                out[row : row + count, :] = lines[...]


def own_kernel(rows, b, cr, trace, coef, sems):
    copies = []
    for h in range(trace.shape[0]):
        lanes = pl.ds(h * LANES, LANES)
        copies.append(
            pltpu.make_async_copy(b.at[:, lanes], trace.at[h, pl.ds(SUB + HALO, rows)], sems.at[2 * h])
        )
        copies.append(pltpu.make_async_copy(cr.at[:, lanes], coef.at[h, pl.ds(HALO, rows)], sems.at[2 * h + 1]))
    for copy in copies:
        copy.start()
    for copy in copies:
        copy.wait()


STATE = ("trace", "coef", "taps", *STAGES, "sums")


def step_kernel(rows, opening, closing, work, fills, coefs, count, *refs):
    refs = list(refs)
    mail = refs[:count]
    refs = refs[count:]
    refs = refs[2 if work["starts"] else len(STATE) :]
    state = dict(zip(STATE, refs, strict=False))
    rest = refs[len(STATE) :]
    trace, coef, taps = state["trace"], state["coef"], state["taps"]
    groups = trace.shape[0]
    frame = rows + 2 * HALO

    for h in range(groups):
        lanes = slice(h * LANES, (h + 1) * LANES)
        for edge, m, row in opening:
            at = 0 if edge == "head" else HALO + rows
            trace[h, SUB + at : SUB + at + HALO, :] = mail[m][row : row + HALO, lanes]
            at = HALO - SPAN if edge == "head" else HALO + rows
            coef[h, at : at + SPAN, :] = mail[m][row + HALO : row + HALO + SPAN, lanes]

    share, offs = rest[-2:]
    for m, row, low, high, first in fills:
        for line in range(low // LANES, -(-high // LANES)):
            a, b = max(low, line * LANES), min(high, (line + 1) * LANES)
            at, skip, size = first + a - low, a - line * LANES, b - a
            for target, lane in ((share, 0), (offs, LANES)):
                values = mail[m][row + line : row + line + 1, lane : lane + LANES]
                square = jnp.broadcast_to(values, (LANES, LANES)).T
                target[at : at + size, :] = square[skip : skip + size]

        def fill(at, step, carry):
            part, off = share[at : at + step, :], offs[at : at + step, :]
            for j, k in enumerate(TAPS):
                taps[j, at + SUB : at + SUB + step, :] = jnp.where(
                    off == k, part, jnp.where(off == k - 1, 1.0 - part, 0.0)
                )
            return carry

        for_chunks([(first, first + high - low)], fill)

    def plain_project(source, target):
        def body(at, step, carry):
            for h, value in enumerate(project(taps, source, at, step)):
                target[h, at + SUB : at + SUB + step, :] = value
            return carry

        return body

    def respond(source, target, ranges):
        for m, row, first, end in coefs:
            def body(at, step, carry, m=m, row=row, first=first):
                mid, total = around(source, at, step)
                for h in range(groups):
                    scale = mail[m][row + at - first : row + at - first + step, h * LANES : (h + 1) * LANES]
                    target[h, at + SUB : at + SUB + step, :] = scale * mid[h] - 0.25 * total[h]
                return carry

            for_chunks([(max(a, first), min(b, end)) for a, b in ranges if max(a, first) < min(b, end)], body)

    def apply(source, response, at, step):
        mid, total = around(source, at, step)
        acc = [coef[h, at : at + step, :] * mid[h] - 0.25 * total[h] for h in range(groups)]
        return mid, give_back(taps, response, at, step, acc)

    def first_image(at, step, carry):
        for h, value in enumerate(apply(trace, state["resp"], at, step)[1]):
            state["image"][h, at + SUB : at + SUB + step, :] = value
        return carry

    def second_image(at, step, carry):
        mid, acc = apply(state["image"], state["resp_two"], at, step)
        carry = list(carry)
        for h in range(groups):
            state["second"][h, at - HALO : at - HALO + step, :] = acc[h]
            right = trace[h, at + SUB : at + SUB + step, :]
            pairs = ((right, mid[h]), (right, acc[h]), (mid[h], mid[h]), (mid[h], acc[h]), (acc[h], acc[h]))
            for j, (u, v) in enumerate(pairs):
                carry[j] = carry[j] + jnp.sum((u * v).reshape(step // SUB, SUB, LANES), axis=0)
        return carry

    for_chunks(work["proj"], plain_project(trace, state["proj"]))
    respond(state["proj"], state["resp"], work["resp"])
    for_chunks(work["image"], first_image)
    for_chunks(work["proj_two"], plain_project(state["image"], state["proj_two"]))
    respond(state["proj_two"], state["resp_two"], work["resp_two"])
    if work["starts"]:
        totals = [jnp.zeros((SUB, LANES), jnp.float32)] * 5
    else:
        totals = [state["sums"][j] for j in range(5)]
    totals = for_chunks(work["second"], second_image, totals)
    if closing:
        lane = lax.broadcasted_iota(jnp.int32, (SUB, LANES), 1)
        line = jnp.zeros((SUB, LANES), jnp.float32)
        for j, total in enumerate(totals):
            line = jnp.where(lane == j, jnp.sum(total), line)
        rest[0][...] = jnp.broadcast_to(line[0:1], rest[0].shape)
    else:
        for j, total in enumerate(totals):
            state["sums"][j] = total
    del frame


def finish_kernel(rows, groups, parts, trace, image, second, solution_out, residual_out, sol, res, sems):
    total = jnp.sum(parts[...], axis=0, keepdims=True)
    b_p, b_q, p_p, p_q, q_q = (total[:, j : j + 1] for j in range(5))
    det = p_p * q_q - p_q * p_q
    y1 = (q_q * b_p - p_q * b_q) / det
    y2 = (p_p * b_q - p_q * b_p) / det
    copies = []
    for i in range(WRITES):
        step = rows // WRITES
        at = i * step
        one = jnp.broadcast_to(y1, (step, LANES))
        two = jnp.broadcast_to(y2, (step, LANES))
        for h in range(groups):
            lanes = slice(h * LANES, (h + 1) * LANES)
            b = trace[h, at + SUB + HALO : at + SUB + HALO + step, :]
            p = image[h, at + SUB + HALO : at + SUB + HALO + step, :]
            q = second[h, at : at + step, :]
            sol[at : at + step, lanes] = one * b + two * p
            res[at : at + step, lanes] = b - one * p - two * q
        for j, (src, dst) in enumerate(((sol, solution_out), (res, residual_out))):
            copy = pltpu.make_async_copy(
                src.at[pl.ds(at, step)], dst.at[pl.ds(at, step)], sems.at[i, j]
            )
            copy.start()
            copies.append(copy)
    for copy in copies:
        copy.wait()


def local(right_side, coef_rotor, coef_stator, mortar_rows, mortar_weight):
    rows, cols = right_side.shape
    groups = cols // LANES
    count = lax.axis_size("circ")
    devices = count * lax.axis_size("radax")
    total_rows = rows * count
    frame = rows + 2 * HALO
    held = frame + 2 * SUB
    whole, remainder = divmod(SLIDE, rows)
    assert cols == W and rows % (WRITES * SUB) == 0 and remainder % SUB == 0
    assert HALO <= remainder <= rows - HALO

    assert rows % LANES == 0

    cut = remainder + HALO
    count_lines = rows // LANES
    spare = HALO - SPAN - REACH - 1
    assert count_lines <= spare
    later = cut + up8((frame - cut) * LATER[0][0] // LATER[0][1])
    middle = cut - up8(cut * LATER[1][0] // LATER[1][1])
    lines_above = frame - later - count_lines
    below, above = whole + 1, whole

    def stator_rows(first, last, low):
        return ("coef", [("stator", first - low, last - first, 0)], first, last)

    low_below, low_above = cut - rows, cut
    edge = ("tail", [("trace", 0, HALO, 0), ("rotor", 0, SPAN, HALO)])
    start = ("head", [("trace", rows - HALO, HALO, 0), ("rotor", rows - SPAN, SPAN, HALO)])
    sent = [
        (above, [stator_rows(later, frame, low_above), ("lines", lines_above, 0, rows - cut + 2 * HALO, cut)]),
        (below, [stator_rows(0, middle, low_below), ("lines", 0, rows - cut, rows, 0)]),
        (below, [stator_rows(middle, cut, low_below)]),
        (above, [stator_rows(cut, later, low_above)]),
        (1, [start]),
    ]
    if (below + 1) % count == 0:
        sent[1][1].append(edge)
    else:
        sent.append((-1, [edge]))
    messages, holds, heights = [], [], []
    for by, parts in sent:
        row, laid = 0, []
        for kind, what, *_ in parts:
            if kind == "lines":
                laid.append((kind, what, None))
                continue
            laid.append((kind, row, what))
            row += up8(sum(size for _, _, size, _ in what))
        messages.append((by, laid))
        holds.append([(kind, at, rest) for (kind, at, _), (_, _, *rest) in zip(laid, parts, strict=True)])
        heights.append(row)
    copies = sum(len(what) for _, laid in messages for kind, _, what in laid if kind != "lines")
    packed = pl.pallas_call(
        functools.partial(pack_kernel, rows, total_rows, messages),
        out_shape=[vmem(height, cols) for height in heights],
        in_specs=[pl.BlockSpec(memory_space=pltpu.HBM)] * 5,
        out_specs=[VMEM] * len(messages),
        scratch_shapes=[
            pltpu.VMEM((count_lines, LANES), jnp.int32),
            vmem(count_lines, LANES),
            vmem(count_lines, cols),
            pltpu.SemaphoreType.DMA((copies + 2,)),
        ],
        compiler_params=PARAMS,
        name="pack",
    )(
        *(
            pltpu.with_memory_space_constraint(x, pltpu.HBM)
            for x in (
                right_side,
                coef_rotor,
                coef_stator,
                mortar_rows.reshape(count_lines, LANES),
                mortar_weight.reshape(count_lines, LANES),
            )
        )
    )
    arrived = [shifted(block, by) for block, (by, _) in zip(packed, messages, strict=True)]

    own = np.zeros(frame, bool)
    own[HALO : HALO + rows] = True
    known = {"trace": own.copy(), "coef": np.zeros(frame, bool), "taps": np.zeros(frame, bool)}
    done = {name: np.zeros(frame, bool) for name in STAGES}
    want = needed(own)
    coefs = []
    shapes = {name: vmem(groups, held, LANES) for name in STATE}
    shapes["coef"] = vmem(groups, frame, LANES)
    shapes["taps"] = vmem(len(TAPS), held, LANES)
    shapes["second"] = vmem(groups, rows, LANES)
    shapes["sums"] = vmem(5, SUB, LANES)

    steps = [[1, 2], [0], list(range(3, len(sent)))]
    taken = []
    state = pl.pallas_call(
        functools.partial(own_kernel, rows),
        out_shape=[shapes["trace"], shapes["coef"]],
        in_specs=[pl.BlockSpec(memory_space=pltpu.HBM)] * 2,
        out_specs=[VMEM] * 2,
        scratch_shapes=[pltpu.SemaphoreType.DMA((2 * groups,))],
        compiler_params=PARAMS,
        name="own",
    )(*(pltpu.with_memory_space_constraint(x, pltpu.HBM) for x in (right_side, coef_rotor)))
    for number, batch in enumerate(steps):
        opening, fills = [], []
        for m in batch:
            taken.append(m)
            for kind, at, what in holds[m]:
                if kind in ("head", "tail"):
                    opening.append((kind, len(taken) - 1, at))
                    known["trace"][slice(0, HALO) if kind == "head" else slice(frame - HALO, frame)] = True
                elif kind == "lines":
                    low, high, first = what
                    fills.append((len(taken) - 1, at, low, high, first))
                    known["taps"][first : first + high - low] = True
                else:
                    first, last = what
                    coefs.append((len(taken) - 1, at, first, last))
                    known["coef"][max(first, spare) : min(last, frame - spare)] = True
        can = reachable(own, known["trace"], known["coef"], known["taps"])
        work = {"starts": number == 0}
        for name in STAGES:
            whole_tiles = name == "second"
            work[name] = spans(can[name] & want[name] & ~done[name], whole_tiles)
            if whole_tiles:
                for a, b in work[name]:
                    done[name][a:b] = True
            else:
                done[name] |= can[name] & want[name]
        closing = number == len(steps) - 1
        out_shape = [shapes[name] for name in STATE] + [vmem(devices, LANES)] * closing
        inputs = [arrived[m] for m in taken]
        state = pl.pallas_call(
            functools.partial(
                step_kernel, rows, opening, closing, work, fills, list(coefs), len(taken)
            ),
            out_shape=out_shape,
            in_specs=[VMEM] * (len(taken) + len(state)),
            out_specs=[VMEM] * len(out_shape),
            scratch_shapes=[vmem(frame, LANES)] * 2,
            input_output_aliases={len(taken) + i: i for i in range(len(state))},
            compiler_params=PARAMS,
            name=f"step{number}",
        )(*inputs, *state)
    *state, line = state
    assert done["second"][HALO : HALO + rows].all()
    state = dict(zip(STATE, state, strict=True))

    parts = lax.all_to_all(line, ("circ", "radax"), 0, 0, tiled=True)

    return pl.pallas_call(
        functools.partial(finish_kernel, rows, groups),
        out_shape=[jax.ShapeDtypeStruct((rows, cols), jnp.float32)] * 2,
        in_specs=[VMEM] * 4,
        out_specs=[pl.BlockSpec(memory_space=pl.ANY)] * 2,
        scratch_shapes=[
            vmem(rows, cols),
            vmem(rows, cols),
            pltpu.SemaphoreType.DMA((WRITES, 2)),
        ],
        compiler_params=PARAMS,
        name="finish",
    )(parts, state["trace"], state["image"], state["second"])


def solution(mesh):
    return jax.shard_map(
        local,
        mesh=mesh,
        in_specs=(P("circ", "radax"), P("circ", "radax"), P("circ", "radax"), P("circ"), P("circ")),
        out_specs=(P("circ", "radax"), P("circ", "radax")),
        check_vma=False,
    )
```

```python
import functools

import jax
import jax.numpy as jnp
import numpy as np
from jax import lax
from jax.experimental import pallas as pl
from jax.experimental.pallas import tpu as pltpu
from jax.sharding import PartitionSpec as P

W = 256
REACH = 3
SLIDE = 1280

LANES = 128
SUB = 8
SPAN = 2 * (REACH + 1)
HALO = 2 * SPAN
TAPS = range(-REACH, REACH + 2)
CHUNK = 64
WRITES = 4
LATER = (1, 4), (1, 2)
VMEM = pl.BlockSpec(memory_space=pltpu.VMEM)
PARAMS = pltpu.CompilerParams(vmem_limit_bytes=40 << 20)


def up8(count):
    return -(-count // SUB) * SUB


def vmem(*shape):
    return pltpu.VMEM(shape, jnp.float32)


def shifted(block, distance):
    count = lax.axis_size("circ")
    route = [((i - distance) % count, i) for i in range(count)]
    return lax.ppermute(block, "circ", route)


def near(mask, low, high):
    out = np.ones_like(mask)
    for k in range(low, high + 1):
        moved = np.zeros_like(mask)
        moved[max(0, -k) : len(mask) - max(0, k)] = mask[max(0, k) : len(mask) - max(0, -k)]
        out &= moved
    return out


def spread(mask, low, high):
    return ~near(~mask, -high, -low)


STAGES = ("proj", "resp", "image", "proj_two", "resp_two", "second")


def reachable(own, trace, coef, tap):
    proj = tap & near(trace, TAPS[0], TAPS[-1])
    resp = coef & near(proj, -1, 1)
    image = trace & near(trace, -1, 1) & near(resp & tap, -TAPS[-1], -TAPS[0])
    proj_two = tap & near(image, TAPS[0], TAPS[-1])
    resp_two = coef & near(proj_two, -1, 1)
    second = own & near(image, -1, 1) & near(resp_two & tap, -TAPS[-1], -TAPS[0])
    return dict(zip(STAGES, (proj, resp, image, proj_two, resp_two, second), strict=True))


def needed(own):
    resp_two = spread(own, -TAPS[-1], -TAPS[0])
    proj_two = spread(resp_two, -1, 1)
    image = spread(own, -1, 1) | spread(proj_two, TAPS[0], TAPS[-1])
    resp = spread(image, -TAPS[-1], -TAPS[0])
    proj = spread(resp, -1, 1)
    return dict(zip(STAGES, (proj, resp, image, proj_two, resp_two, own), strict=True))


def spans(mask, whole):
    tiles = mask.reshape(-1, SUB)
    tiles = tiles.all(1) if whole else tiles.any(1)
    edges = np.flatnonzero(np.diff(np.concatenate([[0], tiles.astype(np.int8), [0]])))
    return [(int(a) * SUB, int(b) * SUB) for a, b in zip(edges[::2], edges[1::2], strict=True)]


def for_chunks(ranges, body, carry=None):
    for first, last in ranges:
        for at in range(first, last, CHUNK):
            carry = body(at, min(CHUNK, last - at), carry)
    return carry


def beside(parts):
    lane = lax.broadcasted_iota(jnp.int32, parts[0].shape, 1)
    ahead = [pltpu.roll(v, 1, 1) for v in parts]
    after = [pltpu.roll(v, LANES - 1, 1) for v in parts]
    out = []
    for h in range(len(parts)):
        before = ahead[h - 1] if h else jnp.zeros_like(parts[0])
        behind = after[h + 1] if h + 1 < len(parts) else jnp.zeros_like(parts[0])
        out.append(
            jnp.where(lane == 0, before, ahead[h])
            + jnp.where(lane == LANES - 1, behind, after[h])
        )
    return out


def around(field, at, step):
    groups = field.shape[0]
    at += SUB
    mid = [field[h, at : at + step, :] for h in range(groups)]
    side = beside(mid)
    total = [
        side[h] + field[h, at - 1 : at - 1 + step, :] + field[h, at + 1 : at + 1 + step, :]
        for h in range(groups)
    ]
    return mid, total


def project(taps, field, at, step):
    acc = [None] * field.shape[0]
    at += SUB
    for j, k in enumerate(TAPS):
        tap = taps[j, at : at + step, :]
        for h in range(len(acc)):
            term = tap * field[h, at + k : at + k + step, :]
            acc[h] = term if acc[h] is None else acc[h] + term
    return acc


def give_back(taps, field, at, step, acc):
    acc = list(acc)
    at += SUB
    for j, k in enumerate(TAPS):
        tap = taps[j, at - k : at - k + step, :]
        for h in range(len(acc)):
            acc[h] = acc[h] + tap * field[h, at - k : at - k + step, :]
    return acc


def pack_kernel(rows, total_rows, messages, b, cr, cs, mortar, weight, *refs):
    refs = refs[len(refs) - len(messages) - 4 :]
    outs, (mortar_here, weight_here, lines, sems) = refs[: len(messages)], refs[len(messages) :]
    sources = {"trace": b, "rotor": cr, "stator": cs}
    small = [
        pltpu.make_async_copy(mortar, mortar_here, sems.at[-1 + sems.shape[0]]),
        pltpu.make_async_copy(weight, weight_here, sems.at[-2 + sems.shape[0]]),
    ]
    for copy in small:
        copy.start()
    copies = []
    for out, (_, parts) in zip(outs, messages, strict=True):
        for kind, row, what in parts:
            if kind == "lines":
                continue
            for source, low, size, skip in what:
                copy = pltpu.make_async_copy(
                    sources[source].at[pl.ds(low, size)], out.at[pl.ds(row + skip, size)], sems.at[len(copies)]
                )
                copy.start()
                copies.append(copy)
    for copy in small:
        copy.wait()
    count = rows // LANES
    shape = (count, LANES)
    facing = lax.rem(lax.axis_index("circ") * rows + SLIDE, total_rows)
    facing = (
        facing
        + lax.broadcasted_iota(jnp.int32, shape, 0) * LANES
        + lax.broadcasted_iota(jnp.int32, shape, 1)
    )
    offset = mortar_here[...] - jnp.where(facing >= total_rows, facing - total_rows, facing)
    offset = jnp.where(offset > total_rows // 2, offset - total_rows, offset)
    offset = jnp.where(offset < -(total_rows // 2), offset + total_rows, offset)
    lines[:, 0:LANES] = weight_here[...]
    lines[:, LANES : 2 * LANES] = offset.astype(jnp.float32)
    for copy in copies:
        copy.wait()
    for out, (_, parts) in zip(outs, messages, strict=True):
        for kind, row, _ in parts:
            if kind == "lines":
                out[row : row + count, :] = lines[...]


def own_kernel(rows, b, cr, trace, coef, sems):
    copies = []
    for h in range(trace.shape[0]):
        lanes = pl.ds(h * LANES, LANES)
        copies.append(
            pltpu.make_async_copy(b.at[:, lanes], trace.at[h, pl.ds(SUB + HALO, rows)], sems.at[2 * h])
        )
        copies.append(pltpu.make_async_copy(cr.at[:, lanes], coef.at[h, pl.ds(HALO, rows)], sems.at[2 * h + 1]))
    for copy in copies:
        copy.start()
    for copy in copies:
        copy.wait()


STATE = ("trace", "coef", "taps", *STAGES, "sums")


def step_kernel(rows, opening, closing, work, fills, coefs, count, *refs):
    refs = list(refs)
    mail = refs[:count]
    refs = refs[count:]
    refs = refs[2 if work["starts"] else len(STATE) :]
    state = dict(zip(STATE, refs, strict=False))
    rest = refs[len(STATE) :]
    trace, coef, taps = state["trace"], state["coef"], state["taps"]
    groups = trace.shape[0]
    frame = rows + 2 * HALO

    for h in range(groups):
        lanes = slice(h * LANES, (h + 1) * LANES)
        for edge, m, row in opening:
            at = 0 if edge == "head" else HALO + rows
            trace[h, SUB + at : SUB + at + HALO, :] = mail[m][row : row + HALO, lanes]
            at = HALO - SPAN if edge == "head" else HALO + rows
            coef[h, at : at + SPAN, :] = mail[m][row + HALO : row + HALO + SPAN, lanes]

    share, offs = rest[-2:]
    for m, row, low, high, first in fills:
        for line in range(low // LANES, -(-high // LANES)):
            a, b = max(low, line * LANES), min(high, (line + 1) * LANES)
            at, skip, size = first + a - low, a - line * LANES, b - a
            for target, lane in ((share, 0), (offs, LANES)):
                values = mail[m][row + line : row + line + 1, lane : lane + LANES]
                square = jnp.broadcast_to(values, (LANES, LANES)).T
                target[at : at + size, :] = square[skip : skip + size]

        def fill(at, step, carry):
            part, off = share[at : at + step, :], offs[at : at + step, :]
            for j, k in enumerate(TAPS):
                taps[j, at + SUB : at + SUB + step, :] = jnp.where(
                    off == k, part, jnp.where(off == k - 1, 1.0 - part, 0.0)
                )
            return carry

        for_chunks([(first, first + high - low)], fill)

    def plain_project(source, target):
        def body(at, step, carry):
            for h, value in enumerate(project(taps, source, at, step)):
                target[h, at + SUB : at + SUB + step, :] = value
            return carry

        return body

    def respond(source, target, ranges):
        for m, row, first, end in coefs:
            def body(at, step, carry, m=m, row=row, first=first):
                mid, total = around(source, at, step)
                for h in range(groups):
                    scale = mail[m][row + at - first : row + at - first + step, h * LANES : (h + 1) * LANES]
                    target[h, at + SUB : at + SUB + step, :] = scale * mid[h] - 0.25 * total[h]
                return carry

            for_chunks([(max(a, first), min(b, end)) for a, b in ranges if max(a, first) < min(b, end)], body)

    def apply(source, response, at, step):
        mid, total = around(source, at, step)
        acc = [coef[h, at : at + step, :] * mid[h] - 0.25 * total[h] for h in range(groups)]
        return mid, give_back(taps, response, at, step, acc)

    def first_image(at, step, carry):
        for h, value in enumerate(apply(trace, state["resp"], at, step)[1]):
            state["image"][h, at + SUB : at + SUB + step, :] = value
        return carry

    def second_image(at, step, carry):
        mid, acc = apply(state["image"], state["resp_two"], at, step)
        carry = list(carry)
        for h in range(groups):
            state["second"][h, at - HALO : at - HALO + step, :] = acc[h]
            right = trace[h, at + SUB : at + SUB + step, :]
            pairs = ((right, mid[h]), (right, acc[h]), (mid[h], mid[h]), (mid[h], acc[h]), (acc[h], acc[h]))
            for j, (u, v) in enumerate(pairs):
                carry[j] = carry[j] + jnp.sum((u * v).reshape(step // SUB, SUB, LANES), axis=0)
        return carry

    for_chunks(work["proj"], plain_project(trace, state["proj"]))
    respond(state["proj"], state["resp"], work["resp"])
    for_chunks(work["image"], first_image)
    for_chunks(work["proj_two"], plain_project(state["image"], state["proj_two"]))
    respond(state["proj_two"], state["resp_two"], work["resp_two"])
    if work["starts"]:
        totals = [jnp.zeros((SUB, LANES), jnp.float32)] * 5
    else:
        totals = [state["sums"][j] for j in range(5)]
    totals = for_chunks(work["second"], second_image, totals)
    if closing:
        lane = lax.broadcasted_iota(jnp.int32, (SUB, LANES), 1)
        line = jnp.zeros((SUB, LANES), jnp.float32)
        for j, total in enumerate(totals):
            line = jnp.where(lane == j, jnp.sum(total), line)
        rest[0][...] = jnp.broadcast_to(line[0:1], rest[0].shape)
    else:
        for j, total in enumerate(totals):
            state["sums"][j] = total
    del frame


def finish_kernel(rows, groups, parts, trace, image, second, solution_out, residual_out, sol, res, sems):
    total = jnp.sum(parts[...], axis=0, keepdims=True)
    b_p, b_q, p_p, p_q, q_q = (total[:, j : j + 1] for j in range(5))
    det = p_p * q_q - p_q * p_q
    y1 = (q_q * b_p - p_q * b_q) / det
    y2 = (p_p * b_q - p_q * b_p) / det
    copies = []
    for i in range(WRITES):
        step = rows // WRITES
        at = i * step
        one = jnp.broadcast_to(y1, (step, LANES))
        two = jnp.broadcast_to(y2, (step, LANES))
        for h in range(groups):
            lanes = slice(h * LANES, (h + 1) * LANES)
            b = trace[h, at + SUB + HALO : at + SUB + HALO + step, :]
            p = image[h, at + SUB + HALO : at + SUB + HALO + step, :]
            q = second[h, at : at + step, :]
            sol[at : at + step, lanes] = one * b + two * p
            res[at : at + step, lanes] = b - one * p - two * q
        for j, (src, dst) in enumerate(((sol, solution_out), (res, residual_out))):
            copy = pltpu.make_async_copy(
                src.at[pl.ds(at, step)], dst.at[pl.ds(at, step)], sems.at[i, j]
            )
            copy.start()
            copies.append(copy)
    for copy in copies:
        copy.wait()


def local(right_side, coef_rotor, coef_stator, mortar_rows, mortar_weight):
    rows, cols = right_side.shape
    groups = cols // LANES
    count = lax.axis_size("circ")
    devices = count * lax.axis_size("radax")
    total_rows = rows * count
    frame = rows + 2 * HALO
    held = frame + 2 * SUB
    whole, remainder = divmod(SLIDE, rows)
    assert cols == W and rows % (WRITES * SUB) == 0 and remainder % SUB == 0
    assert HALO <= remainder <= rows - HALO

    assert rows % LANES == 0

    cut = remainder + HALO
    count_lines = rows // LANES
    spare = HALO - SPAN - REACH - 1
    assert count_lines <= spare
    later = cut + up8((frame - cut) * LATER[0][0] // LATER[0][1])
    middle = cut - up8(cut * LATER[1][0] // LATER[1][1])
    lines_above = frame - later - count_lines
    below, above = whole + 1, whole

    def stator_rows(first, last, low):
        return ("coef", [("stator", first - low, last - first, 0)], first, last)

    low_below, low_above = cut - rows, cut
    edge = ("tail", [("trace", 0, HALO, 0), ("rotor", 0, SPAN, HALO)])
    start = ("head", [("trace", rows - HALO, HALO, 0), ("rotor", rows - SPAN, SPAN, HALO)])
    sent = [
        (above, [stator_rows(later, frame, low_above), ("lines", lines_above, 0, rows - cut + 2 * HALO, cut)]),
        (below, [stator_rows(0, middle, low_below), ("lines", 0, rows - cut, rows, 0)]),
        (below, [stator_rows(middle, cut, low_below)]),
        (above, [stator_rows(cut, later, low_above)]),
        (1, [start]),
    ]
    if (below + 1) % count == 0:
        sent[1][1].append(edge)
    else:
        sent.append((-1, [edge]))
    messages, holds, heights = [], [], []
    for by, parts in sent:
        row, laid = 0, []
        for kind, what, *_ in parts:
            if kind == "lines":
                laid.append((kind, what, None))
                continue
            laid.append((kind, row, what))
            row += up8(sum(size for _, _, size, _ in what))
        messages.append((by, laid))
        holds.append([(kind, at, rest) for (kind, at, _), (_, _, *rest) in zip(laid, parts, strict=True)])
        heights.append(row)
    sources = [
        pltpu.with_memory_space_constraint(x, pltpu.HBM)
        for x in (
            right_side,
            coef_rotor,
            coef_stator,
            mortar_rows.reshape(count_lines, LANES),
            mortar_weight.reshape(count_lines, LANES),
        )
    ]

    def pack(some, after):
        laid = [messages[m] for m in some]
        copies = sum(len(what) for _, parts in laid for kind, _, what in parts if kind != "lines")
        return pl.pallas_call(
            functools.partial(pack_kernel, rows, total_rows, laid),
            out_shape=[vmem(heights[m], cols) for m in some],
            in_specs=[pl.BlockSpec(memory_space=pltpu.HBM)] * 5 + [VMEM] * len(after),
            out_specs=[VMEM] * len(some),
            scratch_shapes=[
                pltpu.VMEM((count_lines, LANES), jnp.int32),
                vmem(count_lines, LANES),
                vmem(count_lines, cols),
                pltpu.SemaphoreType.DMA((copies + 2,)),
            ],
            compiler_params=PARAMS,
            name="pack",
        )(*sources, *after)

    packed = pack([0], [])
    packed += pack(range(1, len(messages)), packed)
    arrived = [shifted(block, by) for block, (by, _) in zip(packed, messages, strict=True)]

    own = np.zeros(frame, bool)
    own[HALO : HALO + rows] = True
    known = {"trace": own.copy(), "coef": np.zeros(frame, bool), "taps": np.zeros(frame, bool)}
    done = {name: np.zeros(frame, bool) for name in STAGES}
    want = needed(own)
    coefs = []
    shapes = {name: vmem(groups, held, LANES) for name in STATE}
    shapes["coef"] = vmem(groups, frame, LANES)
    shapes["taps"] = vmem(len(TAPS), held, LANES)
    shapes["second"] = vmem(groups, rows, LANES)
    shapes["sums"] = vmem(5, SUB, LANES)

    steps = [[1], [2], [0], list(range(3, len(sent)))]
    taken = []
    state = pl.pallas_call(
        functools.partial(own_kernel, rows),
        out_shape=[shapes["trace"], shapes["coef"]],
        in_specs=[pl.BlockSpec(memory_space=pltpu.HBM)] * 2,
        out_specs=[VMEM] * 2,
        scratch_shapes=[pltpu.SemaphoreType.DMA((2 * groups,))],
        compiler_params=PARAMS,
        name="own",
    )(*(pltpu.with_memory_space_constraint(x, pltpu.HBM) for x in (right_side, coef_rotor)))
    for number, batch in enumerate(steps):
        opening, fills = [], []
        for m in batch:
            taken.append(m)
            for kind, at, what in holds[m]:
                if kind in ("head", "tail"):
                    opening.append((kind, len(taken) - 1, at))
                    known["trace"][slice(0, HALO) if kind == "head" else slice(frame - HALO, frame)] = True
                elif kind == "lines":
                    low, high, first = what
                    fills.append((len(taken) - 1, at, low, high, first))
                    known["taps"][first : first + high - low] = True
                else:
                    first, last = what
                    coefs.append((len(taken) - 1, at, first, last))
                    known["coef"][max(first, spare) : min(last, frame - spare)] = True
        can = reachable(own, known["trace"], known["coef"], known["taps"])
        work = {"starts": number == 0}
        for name in STAGES:
            whole_tiles = name == "second"
            work[name] = spans(can[name] & want[name] & ~done[name], whole_tiles)
            if whole_tiles:
                for a, b in work[name]:
                    done[name][a:b] = True
            else:
                done[name] |= can[name] & want[name]
        closing = number == len(steps) - 1
        out_shape = [shapes[name] for name in STATE] + [vmem(devices, LANES)] * closing
        inputs = [arrived[m] for m in taken]
        state = pl.pallas_call(
            functools.partial(
                step_kernel, rows, opening, closing, work, fills, list(coefs), len(taken)
            ),
            out_shape=out_shape,
            in_specs=[VMEM] * (len(taken) + len(state)),
            out_specs=[VMEM] * len(out_shape),
            scratch_shapes=[vmem(frame, LANES)] * 2,
            input_output_aliases={len(taken) + i: i for i in range(len(state))},
            compiler_params=PARAMS,
            name=f"step{number}",
        )(*inputs, *state)
    *state, line = state
    assert done["second"][HALO : HALO + rows].all()
    state = dict(zip(STATE, state, strict=True))

    parts = lax.all_to_all(line, ("circ", "radax"), 0, 0, tiled=True)

    return pl.pallas_call(
        functools.partial(finish_kernel, rows, groups),
        out_shape=[jax.ShapeDtypeStruct((rows, cols), jnp.float32)] * 2,
        in_specs=[VMEM] * 4,
        out_specs=[pl.BlockSpec(memory_space=pl.ANY)] * 2,
        scratch_shapes=[
            vmem(rows, cols),
            vmem(rows, cols),
            pltpu.SemaphoreType.DMA((WRITES, 2)),
        ],
        compiler_params=PARAMS,
        name="finish",
    )(parts, state["trace"], state["image"], state["second"])


def solution(mesh):
    return jax.shard_map(
        local,
        mesh=mesh,
        in_specs=(P("circ", "radax"), P("circ", "radax"), P("circ", "radax"), P("circ"), P("circ")),
        out_specs=(P("circ", "radax"), P("circ", "radax")),
        check_vma=False,
    )
```

```python
import functools

import jax
import jax.numpy as jnp
import numpy as np
from jax import lax
from jax.experimental import pallas as pl
from jax.experimental.pallas import tpu as pltpu
from jax.sharding import PartitionSpec as P

W = 256
REACH = 3
SLIDE = 1280

LANES = 128
SUB = 8
SPAN = 2 * (REACH + 1)
HALO = 2 * SPAN
TAPS = range(-REACH, REACH + 2)
CHUNK = 16
WRITES = 4
LATER = (1, 4), (1, 2)
VMEM = pl.BlockSpec(memory_space=pltpu.VMEM)
PARAMS = pltpu.CompilerParams(vmem_limit_bytes=40 << 20)


def up8(count):
    return -(-count // SUB) * SUB


def vmem(*shape):
    return pltpu.VMEM(shape, jnp.float32)


def shifted(block, distance):
    count = lax.axis_size("circ")
    route = [((i - distance) % count, i) for i in range(count)]
    return lax.ppermute(block, "circ", route)


def near(mask, low, high):
    out = np.ones_like(mask)
    for k in range(low, high + 1):
        moved = np.zeros_like(mask)
        moved[max(0, -k) : len(mask) - max(0, k)] = mask[max(0, k) : len(mask) - max(0, -k)]
        out &= moved
    return out


def spread(mask, low, high):
    return ~near(~mask, -high, -low)


STAGES = ("proj", "resp", "image", "proj_two", "resp_two", "second")


def reachable(own, trace, coef, tap):
    proj = tap & near(trace, TAPS[0], TAPS[-1])
    resp = coef & near(proj, -1, 1)
    image = trace & near(trace, -1, 1) & near(resp & tap, -TAPS[-1], -TAPS[0])
    proj_two = tap & near(image, TAPS[0], TAPS[-1])
    resp_two = coef & near(proj_two, -1, 1)
    second = own & near(image, -1, 1) & near(resp_two & tap, -TAPS[-1], -TAPS[0])
    return dict(zip(STAGES, (proj, resp, image, proj_two, resp_two, second), strict=True))


def needed(own):
    resp_two = spread(own, -TAPS[-1], -TAPS[0])
    proj_two = spread(resp_two, -1, 1)
    image = spread(own, -1, 1) | spread(proj_two, TAPS[0], TAPS[-1])
    resp = spread(image, -TAPS[-1], -TAPS[0])
    proj = spread(resp, -1, 1)
    return dict(zip(STAGES, (proj, resp, image, proj_two, resp_two, own), strict=True))


def spans(mask, whole):
    tiles = mask.reshape(-1, SUB)
    tiles = tiles.all(1) if whole else tiles.any(1)
    edges = np.flatnonzero(np.diff(np.concatenate([[0], tiles.astype(np.int8), [0]])))
    return [(int(a) * SUB, int(b) * SUB) for a, b in zip(edges[::2], edges[1::2], strict=True)]


def for_chunks(ranges, body, carry=None):
    for first, last in ranges:
        for at in range(first, last, CHUNK):
            carry = body(at, min(CHUNK, last - at), carry)
    return carry


def beside(parts):
    lane = lax.broadcasted_iota(jnp.int32, parts[0].shape, 1)
    ahead = [pltpu.roll(v, 1, 1) for v in parts]
    after = [pltpu.roll(v, LANES - 1, 1) for v in parts]
    out = []
    for h in range(len(parts)):
        before = ahead[h - 1] if h else jnp.zeros_like(parts[0])
        behind = after[h + 1] if h + 1 < len(parts) else jnp.zeros_like(parts[0])
        out.append(
            jnp.where(lane == 0, before, ahead[h])
            + jnp.where(lane == LANES - 1, behind, after[h])
        )
    return out


def around(field, at, step):
    groups = field.shape[0]
    at += SUB
    mid = [field[h, at : at + step, :] for h in range(groups)]
    side = beside(mid)
    total = [
        side[h] + field[h, at - 1 : at - 1 + step, :] + field[h, at + 1 : at + 1 + step, :]
        for h in range(groups)
    ]
    return mid, total


def project(taps, field, at, step):
    acc = [None] * field.shape[0]
    at += SUB
    for j, k in enumerate(TAPS):
        tap = taps[j, at : at + step, :]
        for h in range(len(acc)):
            term = tap * field[h, at + k : at + k + step, :]
            acc[h] = term if acc[h] is None else acc[h] + term
    return acc


def give_back(taps, field, at, step, acc):
    acc = list(acc)
    at += SUB
    for j, k in enumerate(TAPS):
        tap = taps[j, at - k : at - k + step, :]
        for h in range(len(acc)):
            acc[h] = acc[h] + tap * field[h, at - k : at - k + step, :]
    return acc


def pack_kernel(rows, total_rows, messages, b, cr, cs, mortar, weight, *refs):
    refs = refs[len(refs) - len(messages) - 4 :]
    outs, (mortar_here, weight_here, lines, sems) = refs[: len(messages)], refs[len(messages) :]
    sources = {"trace": b, "rotor": cr, "stator": cs}
    small = [
        pltpu.make_async_copy(mortar, mortar_here, sems.at[-1 + sems.shape[0]]),
        pltpu.make_async_copy(weight, weight_here, sems.at[-2 + sems.shape[0]]),
    ]
    for copy in small:
        copy.start()
    copies = []
    for out, (_, parts) in zip(outs, messages, strict=True):
        for kind, row, what in parts:
            if kind == "lines":
                continue
            for source, low, size, skip in what:
                copy = pltpu.make_async_copy(
                    sources[source].at[pl.ds(low, size)], out.at[pl.ds(row + skip, size)], sems.at[len(copies)]
                )
                copy.start()
                copies.append(copy)
    for copy in small:
        copy.wait()
    count = rows // LANES
    shape = (count, LANES)
    facing = lax.rem(lax.axis_index("circ") * rows + SLIDE, total_rows)
    facing = (
        facing
        + lax.broadcasted_iota(jnp.int32, shape, 0) * LANES
        + lax.broadcasted_iota(jnp.int32, shape, 1)
    )
    offset = mortar_here[...] - jnp.where(facing >= total_rows, facing - total_rows, facing)
    offset = jnp.where(offset > total_rows // 2, offset - total_rows, offset)
    offset = jnp.where(offset < -(total_rows // 2), offset + total_rows, offset)
    lines[:, 0:LANES] = weight_here[...]
    lines[:, LANES : 2 * LANES] = offset.astype(jnp.float32)
    for copy in copies:
        copy.wait()
    for out, (_, parts) in zip(outs, messages, strict=True):
        for kind, row, _ in parts:
            if kind == "lines":
                out[row : row + count, :] = lines[...]


def own_kernel(rows, b, cr, trace, coef, sems):
    copies = []
    for h in range(trace.shape[0]):
        lanes = pl.ds(h * LANES, LANES)
        copies.append(
            pltpu.make_async_copy(b.at[:, lanes], trace.at[h, pl.ds(SUB + HALO, rows)], sems.at[2 * h])
        )
        copies.append(pltpu.make_async_copy(cr.at[:, lanes], coef.at[h, pl.ds(HALO, rows)], sems.at[2 * h + 1]))
    for copy in copies:
        copy.start()
    for copy in copies:
        copy.wait()


STATE = ("trace", "coef", "taps", *STAGES, "sums")


def step_kernel(rows, opening, closing, work, fills, coefs, count, *refs):
    refs = list(refs)
    mail = refs[:count]
    refs = refs[count:]
    refs = refs[2 if work["starts"] else len(STATE) :]
    state = dict(zip(STATE, refs, strict=False))
    rest = refs[len(STATE) :]
    trace, coef, taps = state["trace"], state["coef"], state["taps"]
    groups = trace.shape[0]
    frame = rows + 2 * HALO

    for h in range(groups):
        lanes = slice(h * LANES, (h + 1) * LANES)
        for edge, m, row in opening:
            at = 0 if edge == "head" else HALO + rows
            trace[h, SUB + at : SUB + at + HALO, :] = mail[m][row : row + HALO, lanes]
            at = HALO - SPAN if edge == "head" else HALO + rows
            coef[h, at : at + SPAN, :] = mail[m][row + HALO : row + HALO + SPAN, lanes]

    share, offs = rest[-2:]
    for m, row, low, high, first in fills:
        for line in range(low // LANES, -(-high // LANES)):
            a, b = max(low, line * LANES), min(high, (line + 1) * LANES)
            at, skip, size = first + a - low, a - line * LANES, b - a
            for target, lane in ((share, 0), (offs, LANES)):
                values = mail[m][row + line : row + line + 1, lane : lane + LANES]
                square = jnp.broadcast_to(values, (LANES, LANES)).T
                target[at : at + size, :] = square[skip : skip + size]

        def fill(at, step, carry):
            part, off = share[at : at + step, :], offs[at : at + step, :]
            for j, k in enumerate(TAPS):
                taps[j, at + SUB : at + SUB + step, :] = jnp.where(
                    off == k, part, jnp.where(off == k - 1, 1.0 - part, 0.0)
                )
            return carry

        for_chunks([(first, first + high - low)], fill)

    def plain_project(source, target):
        def body(at, step, carry):
            for h, value in enumerate(project(taps, source, at, step)):
                target[h, at + SUB : at + SUB + step, :] = value
            return carry

        return body

    def respond(source, target, ranges):
        for m, row, first, end in coefs:
            def body(at, step, carry, m=m, row=row, first=first):
                mid, total = around(source, at, step)
                for h in range(groups):
                    scale = mail[m][row + at - first : row + at - first + step, h * LANES : (h + 1) * LANES]
                    target[h, at + SUB : at + SUB + step, :] = scale * mid[h] - 0.25 * total[h]
                return carry

            for_chunks([(max(a, first), min(b, end)) for a, b in ranges if max(a, first) < min(b, end)], body)

    def apply(source, response, at, step):
        mid, total = around(source, at, step)
        acc = [coef[h, at : at + step, :] * mid[h] - 0.25 * total[h] for h in range(groups)]
        return mid, give_back(taps, response, at, step, acc)

    def first_image(at, step, carry):
        for h, value in enumerate(apply(trace, state["resp"], at, step)[1]):
            state["image"][h, at + SUB : at + SUB + step, :] = value
        return carry

    def second_image(at, step, carry):
        mid, acc = apply(state["image"], state["resp_two"], at, step)
        carry = list(carry)
        for h in range(groups):
            state["second"][h, at - HALO : at - HALO + step, :] = acc[h]
            right = trace[h, at + SUB : at + SUB + step, :]
            pairs = ((right, mid[h]), (right, acc[h]), (mid[h], mid[h]), (mid[h], acc[h]), (acc[h], acc[h]))
            for j, (u, v) in enumerate(pairs):
                carry[j] = carry[j] + jnp.sum((u * v).reshape(step // SUB, SUB, LANES), axis=0)
        return carry

    for_chunks(work["proj"], plain_project(trace, state["proj"]))
    respond(state["proj"], state["resp"], work["resp"])
    for_chunks(work["image"], first_image)
    for_chunks(work["proj_two"], plain_project(state["image"], state["proj_two"]))
    respond(state["proj_two"], state["resp_two"], work["resp_two"])
    if work["starts"]:
        totals = [jnp.zeros((SUB, LANES), jnp.float32)] * 5
    else:
        totals = [state["sums"][j] for j in range(5)]
    totals = for_chunks(work["second"], second_image, totals)
    if closing:
        lane = lax.broadcasted_iota(jnp.int32, (SUB, LANES), 1)
        line = jnp.zeros((SUB, LANES), jnp.float32)
        for j, total in enumerate(totals):
            line = jnp.where(lane == j, jnp.sum(total), line)
        rest[0][...] = jnp.broadcast_to(line[0:1], rest[0].shape)
    else:
        for j, total in enumerate(totals):
            state["sums"][j] = total
    del frame


def finish_kernel(rows, groups, parts, trace, image, second, solution_out, residual_out, sol, res, sems):
    total = jnp.sum(parts[...], axis=0, keepdims=True)
    b_p, b_q, p_p, p_q, q_q = (total[:, j : j + 1] for j in range(5))
    det = p_p * q_q - p_q * p_q
    y1 = (q_q * b_p - p_q * b_q) / det
    y2 = (p_p * b_q - p_q * b_p) / det
    copies = []
    for i in range(WRITES):
        step = rows // WRITES
        at = i * step
        one = jnp.broadcast_to(y1, (step, LANES))
        two = jnp.broadcast_to(y2, (step, LANES))
        for h in range(groups):
            lanes = slice(h * LANES, (h + 1) * LANES)
            b = trace[h, at + SUB + HALO : at + SUB + HALO + step, :]
            p = image[h, at + SUB + HALO : at + SUB + HALO + step, :]
            q = second[h, at : at + step, :]
            sol[at : at + step, lanes] = one * b + two * p
            res[at : at + step, lanes] = b - one * p - two * q
        for j, (src, dst) in enumerate(((sol, solution_out), (res, residual_out))):
            copy = pltpu.make_async_copy(
                src.at[pl.ds(at, step)], dst.at[pl.ds(at, step)], sems.at[i, j]
            )
            copy.start()
            copies.append(copy)
    for copy in copies:
        copy.wait()


def local(right_side, coef_rotor, coef_stator, mortar_rows, mortar_weight):
    rows, cols = right_side.shape
    groups = cols // LANES
    count = lax.axis_size("circ")
    devices = count * lax.axis_size("radax")
    total_rows = rows * count
    frame = rows + 2 * HALO
    held = frame + 2 * SUB
    whole, remainder = divmod(SLIDE, rows)
    assert cols == W and rows % (WRITES * SUB) == 0 and remainder % SUB == 0
    assert HALO <= remainder <= rows - HALO

    assert rows % LANES == 0

    cut = remainder + HALO
    count_lines = rows // LANES
    spare = HALO - SPAN - REACH - 1
    assert count_lines <= spare
    later = cut + up8((frame - cut) * LATER[0][0] // LATER[0][1])
    middle = cut - up8(cut * LATER[1][0] // LATER[1][1])
    lines_above = frame - later - count_lines
    below, above = whole + 1, whole

    def stator_rows(first, last, low):
        return ("coef", [("stator", first - low, last - first, 0)], first, last)

    low_below, low_above = cut - rows, cut
    edge = ("tail", [("trace", 0, HALO, 0), ("rotor", 0, SPAN, HALO)])
    start = ("head", [("trace", rows - HALO, HALO, 0), ("rotor", rows - SPAN, SPAN, HALO)])
    sent = [
        (above, [stator_rows(later, frame, low_above), ("lines", lines_above, 0, rows - cut + 2 * HALO, cut)]),
        (below, [stator_rows(0, middle, low_below), ("lines", 0, rows - cut, rows, 0)]),
        (below, [stator_rows(middle, cut, low_below)]),
        (above, [stator_rows(cut, later, low_above)]),
        (1, [start]),
    ]
    if (below + 1) % count == 0:
        sent[1][1].append(edge)
    else:
        sent.append((-1, [edge]))
    messages, holds, heights = [], [], []
    for by, parts in sent:
        row, laid = 0, []
        for kind, what, *_ in parts:
            if kind == "lines":
                laid.append((kind, what, None))
                continue
            laid.append((kind, row, what))
            row += up8(sum(size for _, _, size, _ in what))
        messages.append((by, laid))
        holds.append([(kind, at, rest) for (kind, at, _), (_, _, *rest) in zip(laid, parts, strict=True)])
        heights.append(row)
    sources = [
        pltpu.with_memory_space_constraint(x, pltpu.HBM)
        for x in (
            right_side,
            coef_rotor,
            coef_stator,
            mortar_rows.reshape(count_lines, LANES),
            mortar_weight.reshape(count_lines, LANES),
        )
    ]

    def pack(some, after):
        laid = [messages[m] for m in some]
        copies = sum(len(what) for _, parts in laid for kind, _, what in parts if kind != "lines")
        return pl.pallas_call(
            functools.partial(pack_kernel, rows, total_rows, laid),
            out_shape=[vmem(heights[m], cols) for m in some],
            in_specs=[pl.BlockSpec(memory_space=pltpu.HBM)] * 5 + [VMEM] * len(after),
            out_specs=[VMEM] * len(some),
            scratch_shapes=[
                pltpu.VMEM((count_lines, LANES), jnp.int32),
                vmem(count_lines, LANES),
                vmem(count_lines, cols),
                pltpu.SemaphoreType.DMA((copies + 2,)),
            ],
            compiler_params=PARAMS,
            name="pack",
        )(*sources, *after)

    packed = pack([0], [])
    packed += pack(range(1, len(messages)), packed)
    arrived = [shifted(block, by) for block, (by, _) in zip(packed, messages, strict=True)]

    own = np.zeros(frame, bool)
    own[HALO : HALO + rows] = True
    known = {"trace": own.copy(), "coef": np.zeros(frame, bool), "taps": np.zeros(frame, bool)}
    done = {name: np.zeros(frame, bool) for name in STAGES}
    want = needed(own)
    coefs = []
    shapes = {name: vmem(groups, held, LANES) for name in STATE}
    shapes["coef"] = vmem(groups, frame, LANES)
    shapes["taps"] = vmem(len(TAPS), held, LANES)
    shapes["second"] = vmem(groups, rows, LANES)
    shapes["sums"] = vmem(5, SUB, LANES)

    steps = [[1], [2], [0], list(range(3, len(sent)))]
    taken = []
    state = pl.pallas_call(
        functools.partial(own_kernel, rows),
        out_shape=[shapes["trace"], shapes["coef"]],
        in_specs=[pl.BlockSpec(memory_space=pltpu.HBM)] * 2,
        out_specs=[VMEM] * 2,
        scratch_shapes=[pltpu.SemaphoreType.DMA((2 * groups,))],
        compiler_params=PARAMS,
        name="own",
    )(*(pltpu.with_memory_space_constraint(x, pltpu.HBM) for x in (right_side, coef_rotor)))
    for number, batch in enumerate(steps):
        opening, fills = [], []
        for m in batch:
            taken.append(m)
            for kind, at, what in holds[m]:
                if kind in ("head", "tail"):
                    opening.append((kind, len(taken) - 1, at))
                    known["trace"][slice(0, HALO) if kind == "head" else slice(frame - HALO, frame)] = True
                elif kind == "lines":
                    low, high, first = what
                    fills.append((len(taken) - 1, at, low, high, first))
                    known["taps"][first : first + high - low] = True
                else:
                    first, last = what
                    coefs.append((len(taken) - 1, at, first, last))
                    known["coef"][max(first, spare) : min(last, frame - spare)] = True
        can = reachable(own, known["trace"], known["coef"], known["taps"])
        work = {"starts": number == 0}
        for name in STAGES:
            whole_tiles = name == "second"
            work[name] = spans(can[name] & want[name] & ~done[name], whole_tiles)
            if whole_tiles:
                for a, b in work[name]:
                    done[name][a:b] = True
            else:
                done[name] |= can[name] & want[name]
        closing = number == len(steps) - 1
        out_shape = [shapes[name] for name in STATE] + [vmem(devices, LANES)] * closing
        inputs = [arrived[m] for m in taken]
        state = pl.pallas_call(
            functools.partial(
                step_kernel, rows, opening, closing, work, fills, list(coefs), len(taken)
            ),
            out_shape=out_shape,
            in_specs=[VMEM] * (len(taken) + len(state)),
            out_specs=[VMEM] * len(out_shape),
            scratch_shapes=[vmem(frame, LANES)] * 2,
            input_output_aliases={len(taken) + i: i for i in range(len(state))},
            compiler_params=PARAMS,
            name=f"step{number}",
        )(*inputs, *state)
    *state, line = state
    assert done["second"][HALO : HALO + rows].all()
    state = dict(zip(STATE, state, strict=True))

    parts = lax.all_to_all(line, ("circ", "radax"), 0, 0, tiled=True)

    return pl.pallas_call(
        functools.partial(finish_kernel, rows, groups),
        out_shape=[jax.ShapeDtypeStruct((rows, cols), jnp.float32)] * 2,
        in_specs=[VMEM] * 4,
        out_specs=[pl.BlockSpec(memory_space=pl.ANY)] * 2,
        scratch_shapes=[
            vmem(rows, cols),
            vmem(rows, cols),
            pltpu.SemaphoreType.DMA((WRITES, 2)),
        ],
        compiler_params=PARAMS,
        name="finish",
    )(parts, state["trace"], state["image"], state["second"])


def solution(mesh):
    return jax.shard_map(
        local,
        mesh=mesh,
        in_specs=(P("circ", "radax"), P("circ", "radax"), P("circ", "radax"), P("circ"), P("circ")),
        out_specs=(P("circ", "radax"), P("circ", "radax")),
        check_vma=False,
    )
```

```python
import functools

import jax
import jax.numpy as jnp
import numpy as np
from jax import lax
from jax.experimental import pallas as pl
from jax.experimental.pallas import tpu as pltpu
from jax.sharding import PartitionSpec as P

W = 256
REACH = 3
SLIDE = 1280

LANES = 128
SUB = 8
SPAN = 2 * (REACH + 1)
HALO = 2 * SPAN
TAPS = range(-REACH, REACH + 2)
CHUNK = 16
WRITES = 4
LATER = (1, 4), (1, 2)
VMEM = pl.BlockSpec(memory_space=pltpu.VMEM)
PARAMS = pltpu.CompilerParams(vmem_limit_bytes=40 << 20)


def up8(count):
    return -(-count // SUB) * SUB


def vmem(*shape):
    return pltpu.VMEM(shape, jnp.float32)


def shifted(block, distance):
    count = lax.axis_size("circ")
    route = [((i - distance) % count, i) for i in range(count)]
    return lax.ppermute(block, "circ", route)


def near(mask, low, high):
    out = np.ones_like(mask)
    for k in range(low, high + 1):
        moved = np.zeros_like(mask)
        moved[max(0, -k) : len(mask) - max(0, k)] = mask[max(0, k) : len(mask) - max(0, -k)]
        out &= moved
    return out


def spread(mask, low, high):
    return ~near(~mask, -high, -low)


STAGES = ("proj", "resp", "image", "proj_two", "resp_two", "second")


def reachable(own, trace, coef, tap):
    proj = tap & near(trace, TAPS[0], TAPS[-1])
    resp = coef & near(proj, -1, 1)
    image = trace & near(trace, -1, 1) & near(resp & tap, -TAPS[-1], -TAPS[0])
    proj_two = tap & near(image, TAPS[0], TAPS[-1])
    resp_two = coef & near(proj_two, -1, 1)
    second = own & near(image, -1, 1) & near(resp_two & tap, -TAPS[-1], -TAPS[0])
    return dict(zip(STAGES, (proj, resp, image, proj_two, resp_two, second), strict=True))


def needed(own):
    resp_two = spread(own, -TAPS[-1], -TAPS[0])
    proj_two = spread(resp_two, -1, 1)
    image = spread(own, -1, 1) | spread(proj_two, TAPS[0], TAPS[-1])
    resp = spread(image, -TAPS[-1], -TAPS[0])
    proj = spread(resp, -1, 1)
    return dict(zip(STAGES, (proj, resp, image, proj_two, resp_two, own), strict=True))


def spans(mask, whole):
    tiles = mask.reshape(-1, SUB)
    tiles = tiles.all(1) if whole else tiles.any(1)
    edges = np.flatnonzero(np.diff(np.concatenate([[0], tiles.astype(np.int8), [0]])))
    return [(int(a) * SUB, int(b) * SUB) for a, b in zip(edges[::2], edges[1::2], strict=True)]


def clip(ranges, low, high):
    return [(max(a, low), min(b, high)) for a, b in ranges if max(a, low) < min(b, high)]


def for_chunks(ranges, body, carry=None):
    for first, last in ranges:
        for at in range(first, last, CHUNK):
            carry = body(at, min(CHUNK, last - at), carry)
    return carry


def beside(parts):
    lane = lax.broadcasted_iota(jnp.int32, parts[0].shape, 1)
    ahead = [pltpu.roll(v, 1, 1) for v in parts]
    after = [pltpu.roll(v, LANES - 1, 1) for v in parts]
    out = []
    for h in range(len(parts)):
        before = ahead[h - 1] if h else jnp.zeros_like(parts[0])
        behind = after[h + 1] if h + 1 < len(parts) else jnp.zeros_like(parts[0])
        out.append(
            jnp.where(lane == 0, before, ahead[h])
            + jnp.where(lane == LANES - 1, behind, after[h])
        )
    return out


def around(field, at, step):
    groups = field.shape[0]
    at += SUB
    mid = [field[h, at : at + step, :] for h in range(groups)]
    side = beside(mid)
    total = [
        side[h] + field[h, at - 1 : at - 1 + step, :] + field[h, at + 1 : at + 1 + step, :]
        for h in range(groups)
    ]
    return mid, total


def project(taps, field, at, step):
    acc = [None] * field.shape[0]
    at += SUB
    for j, k in enumerate(TAPS):
        tap = taps[j, at : at + step, :]
        for h in range(len(acc)):
            term = tap * field[h, at + k : at + k + step, :]
            acc[h] = term if acc[h] is None else acc[h] + term
    return acc


def give_back(taps, field, at, step, acc):
    acc = list(acc)
    at += SUB
    for j, k in enumerate(TAPS):
        tap = taps[j, at - k : at - k + step, :]
        for h in range(len(acc)):
            acc[h] = acc[h] + tap * field[h, at - k : at - k + step, :]
    return acc


def pack_kernel(rows, total_rows, messages, b, cr, cs, mortar, weight, *refs):
    refs = refs[len(refs) - len(messages) - 4 :]
    outs, (mortar_here, weight_here, lines, sems) = refs[: len(messages)], refs[len(messages) :]
    sources = {"trace": b, "rotor": cr, "stator": cs}
    small = [
        pltpu.make_async_copy(mortar, mortar_here, sems.at[-1 + sems.shape[0]]),
        pltpu.make_async_copy(weight, weight_here, sems.at[-2 + sems.shape[0]]),
    ]
    for copy in small:
        copy.start()
    copies = []
    for out, (_, parts) in zip(outs, messages, strict=True):
        for kind, row, what in parts:
            if kind == "lines":
                continue
            for source, low, size, skip in what:
                copy = pltpu.make_async_copy(
                    sources[source].at[pl.ds(low, size)], out.at[pl.ds(row + skip, size)], sems.at[len(copies)]
                )
                copy.start()
                copies.append(copy)
    for copy in small:
        copy.wait()
    count = rows // LANES
    shape = (count, LANES)
    facing = lax.rem(lax.axis_index("circ") * rows + SLIDE, total_rows)
    facing = (
        facing
        + lax.broadcasted_iota(jnp.int32, shape, 0) * LANES
        + lax.broadcasted_iota(jnp.int32, shape, 1)
    )
    offset = mortar_here[...] - jnp.where(facing >= total_rows, facing - total_rows, facing)
    offset = jnp.where(offset > total_rows // 2, offset - total_rows, offset)
    offset = jnp.where(offset < -(total_rows // 2), offset + total_rows, offset)
    lines[:, 0:LANES] = weight_here[...]
    lines[:, LANES : 2 * LANES] = offset.astype(jnp.float32)
    for copy in copies:
        copy.wait()
    for out, (_, parts) in zip(outs, messages, strict=True):
        for kind, row, _ in parts:
            if kind == "lines":
                out[row : row + count, :] = lines[...]


def inner(rows):
    return HALO + SUB, HALO + rows - SUB


def own_kernel(rows, b, cr, trace, coef, base, sems):
    groups = trace.shape[0]
    copies = []
    for h in range(groups):
        lanes = pl.ds(h * LANES, LANES)
        copies.append(
            pltpu.make_async_copy(b.at[:, lanes], trace.at[h, pl.ds(SUB + HALO, rows)], sems.at[2 * h])
        )
        copies.append(pltpu.make_async_copy(cr.at[:, lanes], coef.at[h, pl.ds(HALO, rows)], sems.at[2 * h + 1]))
    for copy in copies:
        copy.start()
    for copy in copies:
        copy.wait()

    def stencil(at, step, carry):
        mid, total = around(trace, at, step)
        for h in range(groups):
            base[h, at : at + step, :] = coef[h, at : at + step, :] * mid[h] - 0.25 * total[h]
        return carry

    for_chunks([inner(rows)], stencil)


STATE = ("trace", "coef", "base", "taps", *STAGES, "sums")


def step_kernel(rows, opening, closing, work, fills, coefs, count, *refs):
    refs = list(refs)
    mail = refs[:count]
    refs = refs[count:]
    refs = refs[3 if work["starts"] else len(STATE) :]
    state = dict(zip(STATE, refs, strict=False))
    rest = refs[len(STATE) :]
    trace, coef, taps = state["trace"], state["coef"], state["taps"]
    groups = trace.shape[0]
    frame = rows + 2 * HALO

    for h in range(groups):
        lanes = slice(h * LANES, (h + 1) * LANES)
        for edge, m, row in opening:
            at = 0 if edge == "head" else HALO + rows
            trace[h, SUB + at : SUB + at + HALO, :] = mail[m][row : row + HALO, lanes]
            at = HALO - SPAN if edge == "head" else HALO + rows
            coef[h, at : at + SPAN, :] = mail[m][row + HALO : row + HALO + SPAN, lanes]

    share, offs = rest[-2:]
    for m, row, low, high, first in fills:
        for line in range(low // LANES, -(-high // LANES)):
            a, b = max(low, line * LANES), min(high, (line + 1) * LANES)
            at, skip, size = first + a - low, a - line * LANES, b - a
            for target, lane in ((share, 0), (offs, LANES)):
                values = mail[m][row + line : row + line + 1, lane : lane + LANES]
                square = jnp.broadcast_to(values, (LANES, LANES)).T
                target[at : at + size, :] = square[skip : skip + size]

        def fill(at, step, carry):
            part, off = share[at : at + step, :], offs[at : at + step, :]
            for j, k in enumerate(TAPS):
                taps[j, at + SUB : at + SUB + step, :] = jnp.where(
                    off == k, part, jnp.where(off == k - 1, 1.0 - part, 0.0)
                )
            return carry

        for_chunks([(first, first + high - low)], fill)

    def plain_project(source, target):
        def body(at, step, carry):
            for h, value in enumerate(project(taps, source, at, step)):
                target[h, at + SUB : at + SUB + step, :] = value
            return carry

        return body

    def respond(source, target, ranges):
        for m, row, first, end in coefs:
            def body(at, step, carry, m=m, row=row, first=first):
                mid, total = around(source, at, step)
                for h in range(groups):
                    scale = mail[m][row + at - first : row + at - first + step, h * LANES : (h + 1) * LANES]
                    target[h, at + SUB : at + SUB + step, :] = scale * mid[h] - 0.25 * total[h]
                return carry

            for_chunks(clip(ranges, first, end), body)

    def apply(source, response, at, step):
        mid, total = around(source, at, step)
        acc = [coef[h, at : at + step, :] * mid[h] - 0.25 * total[h] for h in range(groups)]
        return mid, give_back(taps, response, at, step, acc)

    def first_image(at, step, carry):
        for h, value in enumerate(apply(trace, state["resp"], at, step)[1]):
            state["image"][h, at + SUB : at + SUB + step, :] = value
        return carry

    def inner_image(at, step, carry):
        acc = [state["base"][h, at : at + step, :] for h in range(groups)]
        for h, value in enumerate(give_back(taps, state["resp"], at, step, acc)):
            state["image"][h, at + SUB : at + SUB + step, :] = value
        return carry

    def second_image(at, step, carry):
        mid, acc = apply(state["image"], state["resp_two"], at, step)
        carry = list(carry)
        for h in range(groups):
            state["second"][h, at - HALO : at - HALO + step, :] = acc[h]
            right = trace[h, at + SUB : at + SUB + step, :]
            pairs = ((right, mid[h]), (right, acc[h]), (mid[h], mid[h]), (mid[h], acc[h]), (acc[h], acc[h]))
            for j, (u, v) in enumerate(pairs):
                carry[j] = carry[j] + jnp.sum((u * v).reshape(step // SUB, SUB, LANES), axis=0)
        return carry

    for_chunks(work["proj"], plain_project(trace, state["proj"]))
    respond(state["proj"], state["resp"], work["resp"])
    low, high = inner(rows)
    for_chunks(clip(work["image"], 0, low) + clip(work["image"], high, frame), first_image)
    for_chunks(clip(work["image"], low, high), inner_image)
    for_chunks(work["proj_two"], plain_project(state["image"], state["proj_two"]))
    respond(state["proj_two"], state["resp_two"], work["resp_two"])
    if work["starts"]:
        totals = [jnp.zeros((SUB, LANES), jnp.float32)] * 5
    else:
        totals = [state["sums"][j] for j in range(5)]
    totals = for_chunks(work["second"], second_image, totals)
    if closing:
        lane = lax.broadcasted_iota(jnp.int32, (SUB, LANES), 1)
        line = jnp.zeros((SUB, LANES), jnp.float32)
        for j, total in enumerate(totals):
            line = jnp.where(lane == j, jnp.sum(total, axis=1, keepdims=True), line)
        rest[0][...] = jnp.broadcast_to(jnp.sum(line, axis=0, keepdims=True), rest[0].shape)
    else:
        for j, total in enumerate(totals):
            state["sums"][j] = total


def finish_kernel(rows, groups, parts, trace, image, second, solution_out, residual_out, sol, res, sems):
    total = jnp.sum(parts[...], axis=0, keepdims=True)
    b_p, b_q, p_p, p_q, q_q = (total[:, j : j + 1] for j in range(5))
    det = p_p * q_q - p_q * p_q
    y1 = (q_q * b_p - p_q * b_q) / det
    y2 = (p_p * b_q - p_q * b_p) / det
    copies = []
    for i in range(WRITES):
        step = rows // WRITES
        at = i * step
        one = jnp.broadcast_to(y1, (step, LANES))
        two = jnp.broadcast_to(y2, (step, LANES))
        for h in range(groups):
            lanes = slice(h * LANES, (h + 1) * LANES)
            b = trace[h, at + SUB + HALO : at + SUB + HALO + step, :]
            p = image[h, at + SUB + HALO : at + SUB + HALO + step, :]
            q = second[h, at : at + step, :]
            sol[at : at + step, lanes] = one * b + two * p
            res[at : at + step, lanes] = b - one * p - two * q
        for j, (src, dst) in enumerate(((sol, solution_out), (res, residual_out))):
            copy = pltpu.make_async_copy(
                src.at[pl.ds(at, step)], dst.at[pl.ds(at, step)], sems.at[i, j]
            )
            copy.start()
            copies.append(copy)
    for copy in copies:
        copy.wait()


def local(right_side, coef_rotor, coef_stator, mortar_rows, mortar_weight):
    rows, cols = right_side.shape
    groups = cols // LANES
    count = lax.axis_size("circ")
    devices = count * lax.axis_size("radax")
    total_rows = rows * count
    frame = rows + 2 * HALO
    held = frame + 2 * SUB
    whole, remainder = divmod(SLIDE, rows)
    assert cols == W and rows % (WRITES * SUB) == 0 and remainder % SUB == 0
    assert HALO <= remainder <= rows - HALO

    assert rows % LANES == 0

    cut = remainder + HALO
    count_lines = rows // LANES
    spare = HALO - SPAN - REACH - 1
    assert count_lines <= spare
    later = cut + up8((frame - cut) * LATER[0][0] // LATER[0][1])
    middle = cut - up8(cut * LATER[1][0] // LATER[1][1])
    lines_above = frame - later - count_lines
    below, above = whole + 1, whole

    def stator_rows(first, last, low):
        return ("coef", [("stator", first - low, last - first, 0)], first, last)

    low_below, low_above = cut - rows, cut
    edge = ("tail", [("trace", 0, HALO, 0), ("rotor", 0, SPAN, HALO)])
    start = ("head", [("trace", rows - HALO, HALO, 0), ("rotor", rows - SPAN, SPAN, HALO)])
    sent = [
        (above, [stator_rows(later, frame, low_above), ("lines", lines_above, 0, rows - cut + 2 * HALO, cut)]),
        (below, [stator_rows(0, middle, low_below), ("lines", 0, rows - cut, rows, 0)]),
        (below, [stator_rows(middle, cut, low_below)]),
        (above, [stator_rows(cut, later, low_above)]),
        (1, [start]),
    ]
    if (below + 1) % count == 0:
        sent[1][1].append(edge)
    else:
        sent.append((-1, [edge]))
    messages, holds, heights = [], [], []
    for by, parts in sent:
        row, laid = 0, []
        for kind, what, *_ in parts:
            if kind == "lines":
                laid.append((kind, what, None))
                continue
            laid.append((kind, row, what))
            row += up8(sum(size for _, _, size, _ in what))
        messages.append((by, laid))
        holds.append([(kind, at, rest) for (kind, at, _), (_, _, *rest) in zip(laid, parts, strict=True)])
        heights.append(row)
    sources = [
        pltpu.with_memory_space_constraint(x, pltpu.HBM)
        for x in (
            right_side,
            coef_rotor,
            coef_stator,
            mortar_rows.reshape(count_lines, LANES),
            mortar_weight.reshape(count_lines, LANES),
        )
    ]

    def pack(some, after):
        laid = [messages[m] for m in some]
        copies = sum(len(what) for _, parts in laid for kind, _, what in parts if kind != "lines")
        return pl.pallas_call(
            functools.partial(pack_kernel, rows, total_rows, laid),
            out_shape=[vmem(heights[m], cols) for m in some],
            in_specs=[pl.BlockSpec(memory_space=pltpu.HBM)] * 5 + [VMEM] * len(after),
            out_specs=[VMEM] * len(some),
            scratch_shapes=[
                pltpu.VMEM((count_lines, LANES), jnp.int32),
                vmem(count_lines, LANES),
                vmem(count_lines, cols),
                pltpu.SemaphoreType.DMA((copies + 2,)),
            ],
            compiler_params=PARAMS,
            name="pack",
        )(*sources, *after)

    packed = pack([0], [])
    packed += pack(range(1, len(messages)), packed)
    arrived = [shifted(block, by) for block, (by, _) in zip(packed, messages, strict=True)]

    own = np.zeros(frame, bool)
    own[HALO : HALO + rows] = True
    known = {"trace": own.copy(), "coef": np.zeros(frame, bool), "taps": np.zeros(frame, bool)}
    done = {name: np.zeros(frame, bool) for name in STAGES}
    want = needed(own)
    coefs = []
    shapes = {name: vmem(groups, held, LANES) for name in STATE}
    shapes["coef"] = shapes["base"] = vmem(groups, frame, LANES)
    shapes["taps"] = vmem(len(TAPS), held, LANES)
    shapes["second"] = vmem(groups, rows, LANES)
    shapes["sums"] = vmem(5, SUB, LANES)

    steps = [[1], [2], [0], list(range(3, len(sent)))]
    taken = []
    state = pl.pallas_call(
        functools.partial(own_kernel, rows),
        out_shape=[shapes["trace"], shapes["coef"], shapes["base"]],
        in_specs=[pl.BlockSpec(memory_space=pltpu.HBM)] * 2,
        out_specs=[VMEM] * 3,
        scratch_shapes=[pltpu.SemaphoreType.DMA((2 * groups,))],
        compiler_params=PARAMS,
        name="own",
    )(*(pltpu.with_memory_space_constraint(x, pltpu.HBM) for x in (right_side, coef_rotor)))
    for number, batch in enumerate(steps):
        opening, fills = [], []
        for m in batch:
            taken.append(m)
            for kind, at, what in holds[m]:
                if kind in ("head", "tail"):
                    opening.append((kind, len(taken) - 1, at))
                    known["trace"][slice(0, HALO) if kind == "head" else slice(frame - HALO, frame)] = True
                elif kind == "lines":
                    low, high, first = what
                    fills.append((len(taken) - 1, at, low, high, first))
                    known["taps"][first : first + high - low] = True
                else:
                    first, last = what
                    coefs.append((len(taken) - 1, at, first, last))
                    known["coef"][max(first, spare) : min(last, frame - spare)] = True
        can = reachable(own, known["trace"], known["coef"], known["taps"])
        work = {"starts": number == 0}
        for name in STAGES:
            whole_tiles = name == "second"
            work[name] = spans(can[name] & want[name] & ~done[name], whole_tiles)
            if whole_tiles:
                for a, b in work[name]:
                    done[name][a:b] = True
            else:
                done[name] |= can[name] & want[name]
        closing = number == len(steps) - 1
        out_shape = [shapes[name] for name in STATE] + [vmem(devices, LANES)] * closing
        inputs = [arrived[m] for m in taken]
        state = pl.pallas_call(
            functools.partial(
                step_kernel, rows, opening, closing, work, fills, list(coefs), len(taken)
            ),
            out_shape=out_shape,
            in_specs=[VMEM] * (len(taken) + len(state)),
            out_specs=[VMEM] * len(out_shape),
            scratch_shapes=[vmem(frame, LANES)] * 2,
            input_output_aliases={len(taken) + i: i for i in range(len(state))},
            compiler_params=PARAMS,
            name=f"step{number}",
        )(*inputs, *state)
    *state, line = state
    assert done["second"][HALO : HALO + rows].all()
    state = dict(zip(STATE, state, strict=True))

    parts = lax.all_to_all(line, ("circ", "radax"), 0, 0, tiled=True)

    return pl.pallas_call(
        functools.partial(finish_kernel, rows, groups),
        out_shape=[jax.ShapeDtypeStruct((rows, cols), jnp.float32)] * 2,
        in_specs=[VMEM] * 4,
        out_specs=[pl.BlockSpec(memory_space=pl.ANY)] * 2,
        scratch_shapes=[
            vmem(rows, cols),
            vmem(rows, cols),
            pltpu.SemaphoreType.DMA((WRITES, 2)),
        ],
        compiler_params=PARAMS,
        name="finish",
    )(parts, state["trace"], state["image"], state["second"])


def solution(mesh):
    return jax.shard_map(
        local,
        mesh=mesh,
        in_specs=(P("circ", "radax"), P("circ", "radax"), P("circ", "radax"), P("circ"), P("circ")),
        out_specs=(P("circ", "radax"), P("circ", "radax")),
        check_vma=False,
    )
```

```python
import functools

import jax
import jax.numpy as jnp
import numpy as np
from jax import lax
from jax.experimental import pallas as pl
from jax.experimental.pallas import tpu as pltpu
from jax.sharding import PartitionSpec as P

W = 256
REACH = 3
SLIDE = 1280

LANES = 128
SUB = 8
SPAN = 2 * (REACH + 1)
HALO = 2 * SPAN
TAPS = range(-REACH, REACH + 2)
CHUNK = 16
WRITES = 4
LATER = (1, 5), (1, 2)
VMEM = pl.BlockSpec(memory_space=pltpu.VMEM)
PARAMS = pltpu.CompilerParams(vmem_limit_bytes=40 << 20)


def up8(count):
    return -(-count // SUB) * SUB


def vmem(*shape):
    return pltpu.VMEM(shape, jnp.float32)


def shifted(block, distance):
    count = lax.axis_size("circ")
    route = [((i - distance) % count, i) for i in range(count)]
    return lax.ppermute(block, "circ", route)


def near(mask, low, high):
    out = np.ones_like(mask)
    for k in range(low, high + 1):
        moved = np.zeros_like(mask)
        moved[max(0, -k) : len(mask) - max(0, k)] = mask[max(0, k) : len(mask) - max(0, -k)]
        out &= moved
    return out


def spread(mask, low, high):
    return ~near(~mask, -high, -low)


STAGES = ("proj", "resp", "image", "proj_two", "resp_two", "second")


def reachable(own, trace, coef, tap):
    proj = tap & near(trace, TAPS[0], TAPS[-1])
    resp = coef & near(proj, -1, 1)
    image = trace & near(trace, -1, 1) & near(resp & tap, -TAPS[-1], -TAPS[0])
    proj_two = tap & near(image, TAPS[0], TAPS[-1])
    resp_two = coef & near(proj_two, -1, 1)
    second = own & near(image, -1, 1) & near(resp_two & tap, -TAPS[-1], -TAPS[0])
    return dict(zip(STAGES, (proj, resp, image, proj_two, resp_two, second), strict=True))


def needed(own):
    resp_two = spread(own, -TAPS[-1], -TAPS[0])
    proj_two = spread(resp_two, -1, 1)
    image = spread(own, -1, 1) | spread(proj_two, TAPS[0], TAPS[-1])
    resp = spread(image, -TAPS[-1], -TAPS[0])
    proj = spread(resp, -1, 1)
    return dict(zip(STAGES, (proj, resp, image, proj_two, resp_two, own), strict=True))


def spans(mask, whole):
    tiles = mask.reshape(-1, SUB)
    tiles = tiles.all(1) if whole else tiles.any(1)
    edges = np.flatnonzero(np.diff(np.concatenate([[0], tiles.astype(np.int8), [0]])))
    return [(int(a) * SUB, int(b) * SUB) for a, b in zip(edges[::2], edges[1::2], strict=True)]


def clip(ranges, low, high):
    return [(max(a, low), min(b, high)) for a, b in ranges if max(a, low) < min(b, high)]


def for_chunks(ranges, body, carry=None):
    for first, last in ranges:
        for at in range(first, last, CHUNK):
            carry = body(at, min(CHUNK, last - at), carry)
    return carry


def beside(parts):
    lane = lax.broadcasted_iota(jnp.int32, parts[0].shape, 1)
    ahead = [pltpu.roll(v, 1, 1) for v in parts]
    after = [pltpu.roll(v, LANES - 1, 1) for v in parts]
    out = []
    for h in range(len(parts)):
        before = ahead[h - 1] if h else jnp.zeros_like(parts[0])
        behind = after[h + 1] if h + 1 < len(parts) else jnp.zeros_like(parts[0])
        out.append(
            jnp.where(lane == 0, before, ahead[h])
            + jnp.where(lane == LANES - 1, behind, after[h])
        )
    return out


def around(field, at, step):
    groups = field.shape[0]
    at += SUB
    mid = [field[h, at : at + step, :] for h in range(groups)]
    side = beside(mid)
    total = [
        side[h] + field[h, at - 1 : at - 1 + step, :] + field[h, at + 1 : at + 1 + step, :]
        for h in range(groups)
    ]
    return mid, total


def project(taps, field, at, step):
    acc = [None] * field.shape[0]
    at += SUB
    for j, k in enumerate(TAPS):
        tap = taps[j, at : at + step, :]
        for h in range(len(acc)):
            term = tap * field[h, at + k : at + k + step, :]
            acc[h] = term if acc[h] is None else acc[h] + term
    return acc


def give_back(taps, field, at, step, acc):
    acc = list(acc)
    at += SUB
    for j, k in enumerate(TAPS):
        tap = taps[j, at - k : at - k + step, :]
        for h in range(len(acc)):
            acc[h] = acc[h] + tap * field[h, at - k : at - k + step, :]
    return acc


def pack_kernel(rows, total_rows, messages, b, cr, cs, mortar, weight, *refs):
    refs = refs[len(refs) - len(messages) - 4 :]
    outs, (mortar_here, weight_here, lines, sems) = refs[: len(messages)], refs[len(messages) :]
    sources = {"trace": b, "rotor": cr, "stator": cs}
    small = [
        pltpu.make_async_copy(mortar, mortar_here, sems.at[-1 + sems.shape[0]]),
        pltpu.make_async_copy(weight, weight_here, sems.at[-2 + sems.shape[0]]),
    ]
    for copy in small:
        copy.start()
    copies = []
    for out, (_, parts) in zip(outs, messages, strict=True):
        for kind, row, what in parts:
            if kind == "lines":
                continue
            for source, low, size, skip in what:
                copy = pltpu.make_async_copy(
                    sources[source].at[pl.ds(low, size)], out.at[pl.ds(row + skip, size)], sems.at[len(copies)]
                )
                copy.start()
                copies.append(copy)
    for copy in small:
        copy.wait()
    count = rows // LANES
    shape = (count, LANES)
    facing = lax.rem(lax.axis_index("circ") * rows + SLIDE, total_rows)
    facing = (
        facing
        + lax.broadcasted_iota(jnp.int32, shape, 0) * LANES
        + lax.broadcasted_iota(jnp.int32, shape, 1)
    )
    offset = mortar_here[...] - jnp.where(facing >= total_rows, facing - total_rows, facing)
    offset = jnp.where(offset > total_rows // 2, offset - total_rows, offset)
    offset = jnp.where(offset < -(total_rows // 2), offset + total_rows, offset)
    lines[:, 0:LANES] = weight_here[...]
    lines[:, LANES : 2 * LANES] = offset.astype(jnp.float32)
    for copy in copies:
        copy.wait()
    for out, (_, parts) in zip(outs, messages, strict=True):
        for kind, row, _ in parts:
            if kind == "lines":
                out[row : row + count, :] = lines[...]


def inner(rows):
    return HALO + SUB, HALO + rows - SUB


def own_kernel(rows, b, cr, trace, coef, base, sems):
    groups = trace.shape[0]
    copies = []
    for h in range(groups):
        lanes = pl.ds(h * LANES, LANES)
        copies.append(
            pltpu.make_async_copy(b.at[:, lanes], trace.at[h, pl.ds(SUB + HALO, rows)], sems.at[2 * h])
        )
        copies.append(pltpu.make_async_copy(cr.at[:, lanes], coef.at[h, pl.ds(HALO, rows)], sems.at[2 * h + 1]))
    for copy in copies:
        copy.start()
    for copy in copies:
        copy.wait()

    def stencil(at, step, carry):
        mid, total = around(trace, at, step)
        for h in range(groups):
            base[h, at : at + step, :] = coef[h, at : at + step, :] * mid[h] - 0.25 * total[h]
        return carry

    for_chunks([inner(rows)], stencil)


STATE = ("trace", "coef", "base", "taps", *STAGES, "sums")


def step_kernel(rows, opening, closing, work, fills, coefs, count, *refs):
    refs = list(refs)
    mail = refs[:count]
    refs = refs[count:]
    refs = refs[3 if work["starts"] else len(STATE) :]
    state = dict(zip(STATE, refs, strict=False))
    rest = refs[len(STATE) :]
    trace, coef, taps = state["trace"], state["coef"], state["taps"]
    groups = trace.shape[0]
    frame = rows + 2 * HALO

    for h in range(groups):
        lanes = slice(h * LANES, (h + 1) * LANES)
        for edge, m, row in opening:
            at = 0 if edge == "head" else HALO + rows
            trace[h, SUB + at : SUB + at + HALO, :] = mail[m][row : row + HALO, lanes]
            at = HALO - SPAN if edge == "head" else HALO + rows
            coef[h, at : at + SPAN, :] = mail[m][row + HALO : row + HALO + SPAN, lanes]

    share, offs = rest[-2:]
    for m, row, low, high, first in fills:
        for line in range(low // LANES, -(-high // LANES)):
            a, b = max(low, line * LANES), min(high, (line + 1) * LANES)
            at, skip, size = first + a - low, a - line * LANES, b - a
            for target, lane in ((share, 0), (offs, LANES)):
                values = mail[m][row + line : row + line + 1, lane : lane + LANES]
                square = jnp.broadcast_to(values, (LANES, LANES)).T
                target[at : at + size, :] = square[skip : skip + size]

        def fill(at, step, carry):
            part, off = share[at : at + step, :], offs[at : at + step, :]
            for j, k in enumerate(TAPS):
                taps[j, at + SUB : at + SUB + step, :] = jnp.where(
                    off == k, part, jnp.where(off == k - 1, 1.0 - part, 0.0)
                )
            return carry

        for_chunks([(first, first + high - low)], fill)

    def plain_project(source, target):
        def body(at, step, carry):
            for h, value in enumerate(project(taps, source, at, step)):
                target[h, at + SUB : at + SUB + step, :] = value
            return carry

        return body

    def respond(source, target, ranges):
        for m, row, first, end in coefs:
            def body(at, step, carry, m=m, row=row, first=first):
                mid, total = around(source, at, step)
                for h in range(groups):
                    scale = mail[m][row + at - first : row + at - first + step, h * LANES : (h + 1) * LANES]
                    target[h, at + SUB : at + SUB + step, :] = scale * mid[h] - 0.25 * total[h]
                return carry

            for_chunks(clip(ranges, first, end), body)

    def apply(source, response, at, step):
        mid, total = around(source, at, step)
        acc = [coef[h, at : at + step, :] * mid[h] - 0.25 * total[h] for h in range(groups)]
        return mid, give_back(taps, response, at, step, acc)

    def first_image(at, step, carry):
        for h, value in enumerate(apply(trace, state["resp"], at, step)[1]):
            state["image"][h, at + SUB : at + SUB + step, :] = value
        return carry

    def inner_image(at, step, carry):
        acc = [state["base"][h, at : at + step, :] for h in range(groups)]
        for h, value in enumerate(give_back(taps, state["resp"], at, step, acc)):
            state["image"][h, at + SUB : at + SUB + step, :] = value
        return carry

    def second_image(at, step, carry):
        mid, acc = apply(state["image"], state["resp_two"], at, step)
        carry = list(carry)
        for h in range(groups):
            state["second"][h, at - HALO : at - HALO + step, :] = acc[h]
            right = trace[h, at + SUB : at + SUB + step, :]
            pairs = ((right, mid[h]), (right, acc[h]), (mid[h], mid[h]), (mid[h], acc[h]), (acc[h], acc[h]))
            for j, (u, v) in enumerate(pairs):
                carry[j] = carry[j] + jnp.sum((u * v).reshape(step // SUB, SUB, LANES), axis=0)
        return carry

    for_chunks(work["proj"], plain_project(trace, state["proj"]))
    respond(state["proj"], state["resp"], work["resp"])
    low, high = inner(rows)
    for_chunks(clip(work["image"], 0, low) + clip(work["image"], high, frame), first_image)
    for_chunks(clip(work["image"], low, high), inner_image)
    for_chunks(work["proj_two"], plain_project(state["image"], state["proj_two"]))
    respond(state["proj_two"], state["resp_two"], work["resp_two"])
    if work["starts"]:
        totals = [jnp.zeros((SUB, LANES), jnp.float32)] * 5
    else:
        totals = [state["sums"][j] for j in range(5)]
    totals = for_chunks(work["second"], second_image, totals)
    if closing:
        lane = lax.broadcasted_iota(jnp.int32, (SUB, LANES), 1)
        line = jnp.zeros((SUB, LANES), jnp.float32)
        for j, total in enumerate(totals):
            line = jnp.where(lane == j, jnp.sum(total, axis=1, keepdims=True), line)
        rest[0][...] = jnp.broadcast_to(jnp.sum(line, axis=0, keepdims=True), rest[0].shape)
    else:
        for j, total in enumerate(totals):
            state["sums"][j] = total


def finish_kernel(rows, groups, parts, trace, image, second, solution_out, residual_out, sol, res, sems):
    total = jnp.sum(parts[...], axis=0, keepdims=True)
    b_p, b_q, p_p, p_q, q_q = (total[:, j : j + 1] for j in range(5))
    det = p_p * q_q - p_q * p_q
    y1 = (q_q * b_p - p_q * b_q) / det
    y2 = (p_p * b_q - p_q * b_p) / det
    copies = []
    for i in range(WRITES):
        step = rows // WRITES
        at = i * step
        one = jnp.broadcast_to(y1, (step, LANES))
        two = jnp.broadcast_to(y2, (step, LANES))
        for h in range(groups):
            lanes = slice(h * LANES, (h + 1) * LANES)
            b = trace[h, at + SUB + HALO : at + SUB + HALO + step, :]
            p = image[h, at + SUB + HALO : at + SUB + HALO + step, :]
            q = second[h, at : at + step, :]
            sol[at : at + step, lanes] = one * b + two * p
            res[at : at + step, lanes] = b - one * p - two * q
        for j, (src, dst) in enumerate(((sol, solution_out), (res, residual_out))):
            copy = pltpu.make_async_copy(
                src.at[pl.ds(at, step)], dst.at[pl.ds(at, step)], sems.at[i, j]
            )
            copy.start()
            copies.append(copy)
    for copy in copies:
        copy.wait()


def local(right_side, coef_rotor, coef_stator, mortar_rows, mortar_weight):
    rows, cols = right_side.shape
    groups = cols // LANES
    count = lax.axis_size("circ")
    devices = count * lax.axis_size("radax")
    total_rows = rows * count
    frame = rows + 2 * HALO
    held = frame + 2 * SUB
    whole, remainder = divmod(SLIDE, rows)
    assert cols == W and rows % (WRITES * SUB) == 0 and remainder % SUB == 0
    assert HALO <= remainder <= rows - HALO

    assert rows % LANES == 0

    cut = remainder + HALO
    count_lines = rows // LANES
    spare = HALO - SPAN - REACH - 1
    assert count_lines <= spare
    later = cut + up8((frame - cut) * LATER[0][0] // LATER[0][1])
    middle = cut - up8(cut * LATER[1][0] // LATER[1][1])
    lines_above = frame - later - count_lines
    below, above = whole + 1, whole

    def stator_rows(first, last, low):
        return ("coef", [("stator", first - low, last - first, 0)], first, last)

    low_below, low_above = cut - rows, cut
    edge = ("tail", [("trace", 0, HALO, 0), ("rotor", 0, SPAN, HALO)])
    start = ("head", [("trace", rows - HALO, HALO, 0), ("rotor", rows - SPAN, SPAN, HALO)])
    sent = [
        (above, [stator_rows(later, frame, low_above), ("lines", lines_above, 0, rows - cut + 2 * HALO, cut)]),
        (below, [stator_rows(0, middle, low_below), ("lines", 0, rows - cut, rows, 0)]),
        (below, [stator_rows(middle, cut, low_below)]),
        (above, [stator_rows(cut, later, low_above)]),
        (1, [start]),
    ]
    if (below + 1) % count == 0:
        sent[1][1].append(edge)
    else:
        sent.append((-1, [edge]))
    messages, holds, heights = [], [], []
    for by, parts in sent:
        row, laid = 0, []
        for kind, what, *_ in parts:
            if kind == "lines":
                laid.append((kind, what, None))
                continue
            laid.append((kind, row, what))
            row += up8(sum(size for _, _, size, _ in what))
        messages.append((by, laid))
        holds.append([(kind, at, rest) for (kind, at, _), (_, _, *rest) in zip(laid, parts, strict=True)])
        heights.append(row)
    sources = [
        pltpu.with_memory_space_constraint(x, pltpu.HBM)
        for x in (
            right_side,
            coef_rotor,
            coef_stator,
            mortar_rows.reshape(count_lines, LANES),
            mortar_weight.reshape(count_lines, LANES),
        )
    ]

    def pack(some, after):
        laid = [messages[m] for m in some]
        copies = sum(len(what) for _, parts in laid for kind, _, what in parts if kind != "lines")
        return pl.pallas_call(
            functools.partial(pack_kernel, rows, total_rows, laid),
            out_shape=[vmem(heights[m], cols) for m in some],
            in_specs=[pl.BlockSpec(memory_space=pltpu.HBM)] * 5 + [VMEM] * len(after),
            out_specs=[VMEM] * len(some),
            scratch_shapes=[
                pltpu.VMEM((count_lines, LANES), jnp.int32),
                vmem(count_lines, LANES),
                vmem(count_lines, cols),
                pltpu.SemaphoreType.DMA((copies + 2,)),
            ],
            compiler_params=PARAMS,
            name="pack",
        )(*sources, *after)

    packed = pack([0], [])
    packed += pack(range(1, len(messages)), packed)
    arrived = [shifted(block, by) for block, (by, _) in zip(packed, messages, strict=True)]

    own = np.zeros(frame, bool)
    own[HALO : HALO + rows] = True
    known = {"trace": own.copy(), "coef": np.zeros(frame, bool), "taps": np.zeros(frame, bool)}
    done = {name: np.zeros(frame, bool) for name in STAGES}
    want = needed(own)
    coefs = []
    shapes = {name: vmem(groups, held, LANES) for name in STATE}
    shapes["coef"] = shapes["base"] = vmem(groups, frame, LANES)
    shapes["taps"] = vmem(len(TAPS), held, LANES)
    shapes["second"] = vmem(groups, rows, LANES)
    shapes["sums"] = vmem(5, SUB, LANES)

    steps = [[1], [2], [0], list(range(3, len(sent)))]
    taken = []
    state = pl.pallas_call(
        functools.partial(own_kernel, rows),
        out_shape=[shapes["trace"], shapes["coef"], shapes["base"]],
        in_specs=[pl.BlockSpec(memory_space=pltpu.HBM)] * 2,
        out_specs=[VMEM] * 3,
        scratch_shapes=[pltpu.SemaphoreType.DMA((2 * groups,))],
        compiler_params=PARAMS,
        name="own",
    )(*(pltpu.with_memory_space_constraint(x, pltpu.HBM) for x in (right_side, coef_rotor)))
    for number, batch in enumerate(steps):
        opening, fills = [], []
        for m in batch:
            taken.append(m)
            for kind, at, what in holds[m]:
                if kind in ("head", "tail"):
                    opening.append((kind, len(taken) - 1, at))
                    known["trace"][slice(0, HALO) if kind == "head" else slice(frame - HALO, frame)] = True
                elif kind == "lines":
                    low, high, first = what
                    fills.append((len(taken) - 1, at, low, high, first))
                    known["taps"][first : first + high - low] = True
                else:
                    first, last = what
                    coefs.append((len(taken) - 1, at, first, last))
                    known["coef"][max(first, spare) : min(last, frame - spare)] = True
        can = reachable(own, known["trace"], known["coef"], known["taps"])
        work = {"starts": number == 0}
        for name in STAGES:
            whole_tiles = name == "second"
            work[name] = spans(can[name] & want[name] & ~done[name], whole_tiles)
            if whole_tiles:
                for a, b in work[name]:
                    done[name][a:b] = True
            else:
                done[name] |= can[name] & want[name]
        closing = number == len(steps) - 1
        out_shape = [shapes[name] for name in STATE] + [vmem(devices, LANES)] * closing
        inputs = [arrived[m] for m in taken]
        state = pl.pallas_call(
            functools.partial(
                step_kernel, rows, opening, closing, work, fills, list(coefs), len(taken)
            ),
            out_shape=out_shape,
            in_specs=[VMEM] * (len(taken) + len(state)),
            out_specs=[VMEM] * len(out_shape),
            scratch_shapes=[vmem(frame, LANES)] * 2,
            input_output_aliases={len(taken) + i: i for i in range(len(state))},
            compiler_params=PARAMS,
            name=f"step{number}",
        )(*inputs, *state)
    *state, line = state
    assert done["second"][HALO : HALO + rows].all()
    state = dict(zip(STATE, state, strict=True))

    parts = lax.all_to_all(line, ("circ", "radax"), 0, 0, tiled=True)

    return pl.pallas_call(
        functools.partial(finish_kernel, rows, groups),
        out_shape=[jax.ShapeDtypeStruct((rows, cols), jnp.float32)] * 2,
        in_specs=[VMEM] * 4,
        out_specs=[pl.BlockSpec(memory_space=pl.ANY)] * 2,
        scratch_shapes=[
            vmem(rows, cols),
            vmem(rows, cols),
            pltpu.SemaphoreType.DMA((WRITES, 2)),
        ],
        compiler_params=PARAMS,
        name="finish",
    )(parts, state["trace"], state["image"], state["second"])


def solution(mesh):
    return jax.shard_map(
        local,
        mesh=mesh,
        in_specs=(P("circ", "radax"), P("circ", "radax"), P("circ", "radax"), P("circ"), P("circ")),
        out_specs=(P("circ", "radax"), P("circ", "radax")),
        check_vma=False,
    )
```

```python
import functools

import jax
import jax.numpy as jnp
import numpy as np
from jax import lax
from jax.experimental import pallas as pl
from jax.experimental.pallas import tpu as pltpu
from jax.sharding import PartitionSpec as P

W = 256
REACH = 3
SLIDE = 1280

LANES = 128
SUB = 8
SPAN = 2 * (REACH + 1)
HALO = 2 * SPAN
TAPS = range(-REACH, REACH + 2)
CHUNK = 16
WRITES = 4
LATER = (1, 5), (3, 8)
VMEM = pl.BlockSpec(memory_space=pltpu.VMEM)
PARAMS = pltpu.CompilerParams(vmem_limit_bytes=40 << 20)


def up8(count):
    return -(-count // SUB) * SUB


def vmem(*shape):
    return pltpu.VMEM(shape, jnp.float32)


def shifted(block, distance):
    count = lax.axis_size("circ")
    route = [((i - distance) % count, i) for i in range(count)]
    return lax.ppermute(block, "circ", route)


def near(mask, low, high):
    out = np.ones_like(mask)
    for k in range(low, high + 1):
        moved = np.zeros_like(mask)
        moved[max(0, -k) : len(mask) - max(0, k)] = mask[max(0, k) : len(mask) - max(0, -k)]
        out &= moved
    return out


def spread(mask, low, high):
    return ~near(~mask, -high, -low)


STAGES = ("proj", "resp", "image", "proj_two", "resp_two", "second")


def reachable(own, trace, coef, tap):
    proj = tap & near(trace, TAPS[0], TAPS[-1])
    resp = coef & near(proj, -1, 1)
    image = trace & near(trace, -1, 1) & near(resp & tap, -TAPS[-1], -TAPS[0])
    proj_two = tap & near(image, TAPS[0], TAPS[-1])
    resp_two = coef & near(proj_two, -1, 1)
    second = own & near(image, -1, 1) & near(resp_two & tap, -TAPS[-1], -TAPS[0])
    return dict(zip(STAGES, (proj, resp, image, proj_two, resp_two, second), strict=True))


def needed(own):
    resp_two = spread(own, -TAPS[-1], -TAPS[0])
    proj_two = spread(resp_two, -1, 1)
    image = spread(own, -1, 1) | spread(proj_two, TAPS[0], TAPS[-1])
    resp = spread(image, -TAPS[-1], -TAPS[0])
    proj = spread(resp, -1, 1)
    return dict(zip(STAGES, (proj, resp, image, proj_two, resp_two, own), strict=True))


def spans(mask, whole):
    tiles = mask.reshape(-1, SUB)
    tiles = tiles.all(1) if whole else tiles.any(1)
    edges = np.flatnonzero(np.diff(np.concatenate([[0], tiles.astype(np.int8), [0]])))
    return [(int(a) * SUB, int(b) * SUB) for a, b in zip(edges[::2], edges[1::2], strict=True)]


def clip(ranges, low, high):
    return [(max(a, low), min(b, high)) for a, b in ranges if max(a, low) < min(b, high)]


def for_chunks(ranges, body, carry=None):
    for first, last in ranges:
        for at in range(first, last, CHUNK):
            carry = body(at, min(CHUNK, last - at), carry)
    return carry


def beside(parts):
    lane = lax.broadcasted_iota(jnp.int32, parts[0].shape, 1)
    ahead = [pltpu.roll(v, 1, 1) for v in parts]
    after = [pltpu.roll(v, LANES - 1, 1) for v in parts]
    out = []
    for h in range(len(parts)):
        before = ahead[h - 1] if h else jnp.zeros_like(parts[0])
        behind = after[h + 1] if h + 1 < len(parts) else jnp.zeros_like(parts[0])
        out.append(
            jnp.where(lane == 0, before, ahead[h])
            + jnp.where(lane == LANES - 1, behind, after[h])
        )
    return out


def around(field, at, step):
    groups = field.shape[0]
    at += SUB
    mid = [field[h, at : at + step, :] for h in range(groups)]
    side = beside(mid)
    total = [
        side[h] + field[h, at - 1 : at - 1 + step, :] + field[h, at + 1 : at + 1 + step, :]
        for h in range(groups)
    ]
    return mid, total


def project(taps, field, at, step):
    acc = [None] * field.shape[0]
    at += SUB
    for j, k in enumerate(TAPS):
        tap = taps[j, at : at + step, :]
        for h in range(len(acc)):
            term = tap * field[h, at + k : at + k + step, :]
            acc[h] = term if acc[h] is None else acc[h] + term
    return acc


def give_back(taps, field, at, step, acc):
    acc = list(acc)
    at += SUB
    for j, k in enumerate(TAPS):
        tap = taps[j, at - k : at - k + step, :]
        for h in range(len(acc)):
            acc[h] = acc[h] + tap * field[h, at - k : at - k + step, :]
    return acc


def pack_kernel(rows, total_rows, messages, b, cr, cs, mortar, weight, *refs):
    refs = refs[len(refs) - len(messages) - 4 :]
    outs, (mortar_here, weight_here, lines, sems) = refs[: len(messages)], refs[len(messages) :]
    sources = {"trace": b, "rotor": cr, "stator": cs}
    small = [
        pltpu.make_async_copy(mortar, mortar_here, sems.at[-1 + sems.shape[0]]),
        pltpu.make_async_copy(weight, weight_here, sems.at[-2 + sems.shape[0]]),
    ]
    for copy in small:
        copy.start()
    copies = []
    for out, (_, parts) in zip(outs, messages, strict=True):
        for kind, row, what in parts:
            if kind == "lines":
                continue
            for source, low, size, skip in what:
                copy = pltpu.make_async_copy(
                    sources[source].at[pl.ds(low, size)], out.at[pl.ds(row + skip, size)], sems.at[len(copies)]
                )
                copy.start()
                copies.append(copy)
    for copy in small:
        copy.wait()
    count = rows // LANES
    shape = (count, LANES)
    facing = lax.rem(lax.axis_index("circ") * rows + SLIDE, total_rows)
    facing = (
        facing
        + lax.broadcasted_iota(jnp.int32, shape, 0) * LANES
        + lax.broadcasted_iota(jnp.int32, shape, 1)
    )
    offset = mortar_here[...] - jnp.where(facing >= total_rows, facing - total_rows, facing)
    offset = jnp.where(offset > total_rows // 2, offset - total_rows, offset)
    offset = jnp.where(offset < -(total_rows // 2), offset + total_rows, offset)
    lines[:, 0:LANES] = weight_here[...]
    lines[:, LANES : 2 * LANES] = offset.astype(jnp.float32)
    for copy in copies:
        copy.wait()
    for out, (_, parts) in zip(outs, messages, strict=True):
        for kind, row, _ in parts:
            if kind == "lines":
                out[row : row + count, :] = lines[...]


def inner(rows):
    return HALO + SUB, HALO + rows - SUB


def own_kernel(rows, b, cr, trace, coef, base, sems):
    groups = trace.shape[0]
    copies = []
    for h in range(groups):
        lanes = pl.ds(h * LANES, LANES)
        copies.append(
            pltpu.make_async_copy(b.at[:, lanes], trace.at[h, pl.ds(SUB + HALO, rows)], sems.at[2 * h])
        )
        copies.append(pltpu.make_async_copy(cr.at[:, lanes], coef.at[h, pl.ds(HALO, rows)], sems.at[2 * h + 1]))
    for copy in copies:
        copy.start()
    for copy in copies:
        copy.wait()

    def stencil(at, step, carry):
        mid, total = around(trace, at, step)
        for h in range(groups):
            base[h, at : at + step, :] = coef[h, at : at + step, :] * mid[h] - 0.25 * total[h]
        return carry

    for_chunks([inner(rows)], stencil)


STATE = ("trace", "coef", "base", "taps", *STAGES, "sums")


def step_kernel(rows, opening, closing, work, fills, coefs, count, *refs):
    refs = list(refs)
    mail = refs[:count]
    refs = refs[count:]
    refs = refs[3 if work["starts"] else len(STATE) :]
    state = dict(zip(STATE, refs, strict=False))
    rest = refs[len(STATE) :]
    trace, coef, taps = state["trace"], state["coef"], state["taps"]
    groups = trace.shape[0]
    frame = rows + 2 * HALO

    for h in range(groups):
        lanes = slice(h * LANES, (h + 1) * LANES)
        for edge, m, row in opening:
            at = 0 if edge == "head" else HALO + rows
            trace[h, SUB + at : SUB + at + HALO, :] = mail[m][row : row + HALO, lanes]
            at = HALO - SPAN if edge == "head" else HALO + rows
            coef[h, at : at + SPAN, :] = mail[m][row + HALO : row + HALO + SPAN, lanes]

    share, offs = rest[-2:]
    for m, row, low, high, first in fills:
        for line in range(low // LANES, -(-high // LANES)):
            a, b = max(low, line * LANES), min(high, (line + 1) * LANES)
            at, skip, size = first + a - low, a - line * LANES, b - a
            for target, lane in ((share, 0), (offs, LANES)):
                values = mail[m][row + line : row + line + 1, lane : lane + LANES]
                square = jnp.broadcast_to(values, (LANES, LANES)).T
                target[at : at + size, :] = square[skip : skip + size]

        def fill(at, step, carry):
            part, off = share[at : at + step, :], offs[at : at + step, :]
            for j, k in enumerate(TAPS):
                taps[j, at + SUB : at + SUB + step, :] = jnp.where(
                    off == k, part, jnp.where(off == k - 1, 1.0 - part, 0.0)
                )
            return carry

        for_chunks([(first, first + high - low)], fill)

    def plain_project(source, target):
        def body(at, step, carry):
            for h, value in enumerate(project(taps, source, at, step)):
                target[h, at + SUB : at + SUB + step, :] = value
            return carry

        return body

    def respond(source, target, ranges):
        for m, row, first, end in coefs:
            def body(at, step, carry, m=m, row=row, first=first):
                mid, total = around(source, at, step)
                for h in range(groups):
                    scale = mail[m][row + at - first : row + at - first + step, h * LANES : (h + 1) * LANES]
                    target[h, at + SUB : at + SUB + step, :] = scale * mid[h] - 0.25 * total[h]
                return carry

            for_chunks(clip(ranges, first, end), body)

    def apply(source, response, at, step):
        mid, total = around(source, at, step)
        acc = [coef[h, at : at + step, :] * mid[h] - 0.25 * total[h] for h in range(groups)]
        return mid, give_back(taps, response, at, step, acc)

    def first_image(at, step, carry):
        for h, value in enumerate(apply(trace, state["resp"], at, step)[1]):
            state["image"][h, at + SUB : at + SUB + step, :] = value
        return carry

    def inner_image(at, step, carry):
        acc = [state["base"][h, at : at + step, :] for h in range(groups)]
        for h, value in enumerate(give_back(taps, state["resp"], at, step, acc)):
            state["image"][h, at + SUB : at + SUB + step, :] = value
        return carry

    def second_image(at, step, carry):
        mid, acc = apply(state["image"], state["resp_two"], at, step)
        carry = list(carry)
        for h in range(groups):
            state["second"][h, at - HALO : at - HALO + step, :] = acc[h]
            right = trace[h, at + SUB : at + SUB + step, :]
            pairs = ((right, mid[h]), (right, acc[h]), (mid[h], mid[h]), (mid[h], acc[h]), (acc[h], acc[h]))
            for j, (u, v) in enumerate(pairs):
                carry[j] = carry[j] + jnp.sum((u * v).reshape(step // SUB, SUB, LANES), axis=0)
        return carry

    for_chunks(work["proj"], plain_project(trace, state["proj"]))
    respond(state["proj"], state["resp"], work["resp"])
    low, high = inner(rows)
    for_chunks(clip(work["image"], 0, low) + clip(work["image"], high, frame), first_image)
    for_chunks(clip(work["image"], low, high), inner_image)
    for_chunks(work["proj_two"], plain_project(state["image"], state["proj_two"]))
    respond(state["proj_two"], state["resp_two"], work["resp_two"])
    if work["starts"]:
        totals = [jnp.zeros((SUB, LANES), jnp.float32)] * 5
    else:
        totals = [state["sums"][j] for j in range(5)]
    totals = for_chunks(work["second"], second_image, totals)
    if closing:
        lane = lax.broadcasted_iota(jnp.int32, (SUB, LANES), 1)
        line = jnp.zeros((SUB, LANES), jnp.float32)
        for j, total in enumerate(totals):
            line = jnp.where(lane == j, jnp.sum(total, axis=1, keepdims=True), line)
        rest[0][...] = jnp.broadcast_to(jnp.sum(line, axis=0, keepdims=True), rest[0].shape)
    else:
        for j, total in enumerate(totals):
            state["sums"][j] = total


def finish_kernel(rows, groups, parts, trace, image, second, solution_out, residual_out, sol, res, sems):
    total = jnp.sum(parts[...], axis=0, keepdims=True)
    b_p, b_q, p_p, p_q, q_q = (total[:, j : j + 1] for j in range(5))
    det = p_p * q_q - p_q * p_q
    y1 = (q_q * b_p - p_q * b_q) / det
    y2 = (p_p * b_q - p_q * b_p) / det
    copies = []
    for i in range(WRITES):
        step = rows // WRITES
        at = i * step
        one = jnp.broadcast_to(y1, (step, LANES))
        two = jnp.broadcast_to(y2, (step, LANES))
        for h in range(groups):
            lanes = slice(h * LANES, (h + 1) * LANES)
            b = trace[h, at + SUB + HALO : at + SUB + HALO + step, :]
            p = image[h, at + SUB + HALO : at + SUB + HALO + step, :]
            q = second[h, at : at + step, :]
            sol[at : at + step, lanes] = one * b + two * p
            res[at : at + step, lanes] = b - one * p - two * q
        for j, (src, dst) in enumerate(((sol, solution_out), (res, residual_out))):
            copy = pltpu.make_async_copy(
                src.at[pl.ds(at, step)], dst.at[pl.ds(at, step)], sems.at[i, j]
            )
            copy.start()
            copies.append(copy)
    for copy in copies:
        copy.wait()


def local(right_side, coef_rotor, coef_stator, mortar_rows, mortar_weight):
    rows, cols = right_side.shape
    groups = cols // LANES
    count = lax.axis_size("circ")
    devices = count * lax.axis_size("radax")
    total_rows = rows * count
    frame = rows + 2 * HALO
    held = frame + 2 * SUB
    whole, remainder = divmod(SLIDE, rows)
    assert cols == W and rows % (WRITES * SUB) == 0 and remainder % SUB == 0
    assert HALO <= remainder <= rows - HALO

    assert rows % LANES == 0

    cut = remainder + HALO
    count_lines = rows // LANES
    spare = HALO - SPAN - REACH - 1
    assert count_lines <= spare
    later = cut + up8((frame - cut) * LATER[0][0] // LATER[0][1])
    middle = cut - up8(cut * LATER[1][0] // LATER[1][1])
    lines_above = frame - later - count_lines
    below, above = whole + 1, whole

    def stator_rows(first, last, low):
        return ("coef", [("stator", first - low, last - first, 0)], first, last)

    low_below, low_above = cut - rows, cut
    edge = ("tail", [("trace", 0, HALO, 0), ("rotor", 0, SPAN, HALO)])
    start = ("head", [("trace", rows - HALO, HALO, 0), ("rotor", rows - SPAN, SPAN, HALO)])
    sent = [
        (above, [stator_rows(later, frame, low_above), ("lines", lines_above, 0, rows - cut + 2 * HALO, cut)]),
        (below, [stator_rows(0, middle, low_below), ("lines", 0, rows - cut, rows, 0)]),
        (below, [stator_rows(middle, cut, low_below)]),
        (above, [stator_rows(cut, later, low_above)]),
        (1, [start]),
    ]
    if (below + 1) % count == 0:
        sent[1][1].append(edge)
    else:
        sent.append((-1, [edge]))
    messages, holds, heights = [], [], []
    for by, parts in sent:
        row, laid = 0, []
        for kind, what, *_ in parts:
            if kind == "lines":
                laid.append((kind, what, None))
                continue
            laid.append((kind, row, what))
            row += up8(sum(size for _, _, size, _ in what))
        messages.append((by, laid))
        holds.append([(kind, at, rest) for (kind, at, _), (_, _, *rest) in zip(laid, parts, strict=True)])
        heights.append(row)
    sources = [
        pltpu.with_memory_space_constraint(x, pltpu.HBM)
        for x in (
            right_side,
            coef_rotor,
            coef_stator,
            mortar_rows.reshape(count_lines, LANES),
            mortar_weight.reshape(count_lines, LANES),
        )
    ]

    def pack(some, after):
        laid = [messages[m] for m in some]
        copies = sum(len(what) for _, parts in laid for kind, _, what in parts if kind != "lines")
        return pl.pallas_call(
            functools.partial(pack_kernel, rows, total_rows, laid),
            out_shape=[vmem(heights[m], cols) for m in some],
            in_specs=[pl.BlockSpec(memory_space=pltpu.HBM)] * 5 + [VMEM] * len(after),
            out_specs=[VMEM] * len(some),
            scratch_shapes=[
                pltpu.VMEM((count_lines, LANES), jnp.int32),
                vmem(count_lines, LANES),
                vmem(count_lines, cols),
                pltpu.SemaphoreType.DMA((copies + 2,)),
            ],
            compiler_params=PARAMS,
            name="pack",
        )(*sources, *after)

    packed = pack([0], [])
    packed += pack(range(1, len(messages)), packed)
    arrived = [shifted(block, by) for block, (by, _) in zip(packed, messages, strict=True)]

    own = np.zeros(frame, bool)
    own[HALO : HALO + rows] = True
    known = {"trace": own.copy(), "coef": np.zeros(frame, bool), "taps": np.zeros(frame, bool)}
    done = {name: np.zeros(frame, bool) for name in STAGES}
    want = needed(own)
    coefs = []
    shapes = {name: vmem(groups, held, LANES) for name in STATE}
    shapes["coef"] = shapes["base"] = vmem(groups, frame, LANES)
    shapes["taps"] = vmem(len(TAPS), held, LANES)
    shapes["second"] = vmem(groups, rows, LANES)
    shapes["sums"] = vmem(5, SUB, LANES)

    steps = [[1], [2], [0], list(range(3, len(sent)))]
    taken = []
    state = pl.pallas_call(
        functools.partial(own_kernel, rows),
        out_shape=[shapes["trace"], shapes["coef"], shapes["base"]],
        in_specs=[pl.BlockSpec(memory_space=pltpu.HBM)] * 2,
        out_specs=[VMEM] * 3,
        scratch_shapes=[pltpu.SemaphoreType.DMA((2 * groups,))],
        compiler_params=PARAMS,
        name="own",
    )(*(pltpu.with_memory_space_constraint(x, pltpu.HBM) for x in (right_side, coef_rotor)))
    for number, batch in enumerate(steps):
        opening, fills = [], []
        for m in batch:
            taken.append(m)
            for kind, at, what in holds[m]:
                if kind in ("head", "tail"):
                    opening.append((kind, len(taken) - 1, at))
                    known["trace"][slice(0, HALO) if kind == "head" else slice(frame - HALO, frame)] = True
                elif kind == "lines":
                    low, high, first = what
                    fills.append((len(taken) - 1, at, low, high, first))
                    known["taps"][first : first + high - low] = True
                else:
                    first, last = what
                    coefs.append((len(taken) - 1, at, first, last))
                    known["coef"][max(first, spare) : min(last, frame - spare)] = True
        can = reachable(own, known["trace"], known["coef"], known["taps"])
        work = {"starts": number == 0}
        for name in STAGES:
            whole_tiles = name == "second"
            work[name] = spans(can[name] & want[name] & ~done[name], whole_tiles)
            if whole_tiles:
                for a, b in work[name]:
                    done[name][a:b] = True
            else:
                done[name] |= can[name] & want[name]
        closing = number == len(steps) - 1
        out_shape = [shapes[name] for name in STATE] + [vmem(devices, LANES)] * closing
        inputs = [arrived[m] for m in taken]
        state = pl.pallas_call(
            functools.partial(
                step_kernel, rows, opening, closing, work, fills, list(coefs), len(taken)
            ),
            out_shape=out_shape,
            in_specs=[VMEM] * (len(taken) + len(state)),
            out_specs=[VMEM] * len(out_shape),
            scratch_shapes=[vmem(frame, LANES)] * 2,
            input_output_aliases={len(taken) + i: i for i in range(len(state))},
            compiler_params=PARAMS,
            name=f"step{number}",
        )(*inputs, *state)
    *state, line = state
    assert done["second"][HALO : HALO + rows].all()
    state = dict(zip(STATE, state, strict=True))

    parts = lax.all_to_all(line, ("circ", "radax"), 0, 0, tiled=True)

    return pl.pallas_call(
        functools.partial(finish_kernel, rows, groups),
        out_shape=[jax.ShapeDtypeStruct((rows, cols), jnp.float32)] * 2,
        in_specs=[VMEM] * 4,
        out_specs=[pl.BlockSpec(memory_space=pl.ANY)] * 2,
        scratch_shapes=[
            vmem(rows, cols),
            vmem(rows, cols),
            pltpu.SemaphoreType.DMA((WRITES, 2)),
        ],
        compiler_params=PARAMS,
        name="finish",
    )(parts, state["trace"], state["image"], state["second"])


def solution(mesh):
    return jax.shard_map(
        local,
        mesh=mesh,
        in_specs=(P("circ", "radax"), P("circ", "radax"), P("circ", "radax"), P("circ"), P("circ")),
        out_specs=(P("circ", "radax"), P("circ", "radax")),
        check_vma=False,
    )
```
